256 devices in a mesh: dp: 16 (over z, y_hi), tensor: 16 (over y_lo, x, core).
Axes of the slice: x: 4, y: 4 (y_hi: 2, y_lo: 2; y = y_hi * 2 + y_lo), z: 8, core: 2. Of those that a mesh axis runs over, the one named last changes fastest.
Arguments:
- tokens: bfloat16 [8192, 4608], P(('dp', 'tensor')), may hold values from -0.7 to 0.7
- norm_gain: float32 [4608], replicated, may hold values from 0.5 to 1.5
- w_query: bfloat16 [4608, 4096], P(None, 'tensor'), may hold values from -0.073656956 to 0.073656956
- w_key: bfloat16 [4608, 2048], P(None, 'tensor'), may hold values from -0.073656956 to 0.073656956
- w_value: bfloat16 [4608, 2048], P(None, 'tensor'), may hold values from -0.09375 to 0.09375
- w_output: bfloat16 [4096, 4608], P('tensor'), may hold values from -0.09375 to 0.09375
- d_mixed: bfloat16 [8192, 4608], P(('dp', 'tensor')), may hold values from -24 to 24
Outputs:
- mixed: bfloat16 [8192, 4608], P(('dp', 'tensor'))
- d_tokens: bfloat16 [8192, 4608], P(('dp', 'tensor'))
- dw_query: float32 [4608, 4096], P('dp', 'tensor')
- dw_key: float32 [4608, 2048], P('dp', 'tensor')
- dw_value: float32 [4608, 2048], P('dp', 'tensor')
- dw_output: float32 [4096, 4608], P('tensor', 'dp')
The draws below stay inside these ranges and needn't reach their ends.
All inputs are finite; a program needn't handle non-finite values.
Results may differ from the reference program's by a relative error of at most 0.025.
Values may be sent and summed in bfloat16 or wider, within the bound.
A program may use at most 128 MiB of HBM per device.

```python
import math
import jax
import jax.numpy as jnp
from jax import lax

D = 4608
HEADS = 32
KV_HEADS = 16
HEAD = 128
SEQ = 512
QD = 4096
KD = 2048
TOKENS = 8192
N_DP = 16
N_TENSOR = 16


def shared_directions(key):
    row_key, head_key = jax.random.split(key)
    feature_signs = (2 * jax.random.randint(row_key, (D,), 0, 2) - 1).astype(jnp.float32)
    head_signs = (2 * jax.random.randint(head_key, (HEAD,), 0, 2) - 1).astype(jnp.float32)
    return (feature_signs, head_signs * HEAD ** (-0.5))


def add_direction(base_part, size_key, feature_signs, head_dir, groups):
    strength = jnp.exp(jax.random.uniform(size_key, (groups,), minval=math.log(0.7), maxval=math.log(1.2)))
    unit_scale = 10.0 * (D // HEADS) ** 0.25 / D
    column = (strength[:, None] * head_dir[None, :]).reshape(groups * HEAD) * unit_scale
    return base_part + feature_signs[:, None] * column[None, :]


def draw_tokens(key, part):
    feature_signs, head_dir = shared_directions(key)
    key = jax.random.fold_in(key, 11)
    noise_key, pick_key, size_key = jax.random.split(key, 3)
    noise_part = jnp.clip(jax.random.normal(noise_key, (TOKENS, D)), -4.0, 4.0)
    chosen = jax.random.randint(pick_key, (TOKENS, 1), 0, 8) == 0
    strength = jax.random.uniform(size_key, (TOKENS, 1), minval=1.0, maxval=3.0)
    lifted = jnp.where(chosen, strength, 0.0) * feature_signs[None, :]
    return (0.1 * (noise_part + lifted)).astype(jnp.bfloat16)


def draw_w_query(key, part):
    feature_signs, head_dir = shared_directions(key)
    key = jax.random.fold_in(key, 12)
    base_key, size_key = jax.random.split(key)
    base_part = jnp.clip(jax.random.normal(base_key, (D, QD)), -4.0, 4.0) * D ** (-0.5)
    return add_direction(base_part, size_key, feature_signs, head_dir, HEADS).astype(jnp.bfloat16)


def draw_w_key(key, part):
    feature_signs, head_dir = shared_directions(key)
    key = jax.random.fold_in(key, 13)
    base_key, size_key = jax.random.split(key)
    base_part = jnp.clip(jax.random.normal(base_key, (D, KD)), -4.0, 4.0) * D ** (-0.5)
    return add_direction(base_part, size_key, feature_signs, head_dir, KV_HEADS).astype(jnp.bfloat16)


def spiked(array, own_key, source, target, shards_of, factor):
    def block_of(dim):
        return (jnp.arange(array.shape[dim]) // (array.shape[dim] // shards_of)).reshape((-1,) + (1,) * (array.ndim - 1 - dim))

    first = jax.random.permutation(own_key, shards_of)[block_of(target)]
    far = (block_of(target) + shards_of // 2) % shards_of
    return jnp.where((block_of(source) == first) | (block_of(source) == far), factor * array, array)


def block_levels(stream_key, shape, cuts, smallest, top_value):
    def one(axis_at, shards_of):
        steps = jax.random.uniform(jax.random.fold_in(jax.random.fold_in(stream_key, 6), axis_at), (shards_of,), jnp.float32, smallest / len(cuts), top_value / len(cuts))
        return jnp.repeat(jnp.exp(steps), shape[axis_at] // shards_of).reshape((-1,) + (1,) * (len(shape) - axis_at - 1))

    factor_of = one(*cuts[0])
    for cut in cuts[1:]:
        factor_of = factor_of * one(*cut)
    return factor_of


def normal_values(own_key, shape, spread, limit, cuts=(), kind=jnp.bfloat16):
    entries = jax.random.normal(own_key, shape, jnp.float32) * spread
    if len(cuts) > 0:
        entries = block_levels(own_key, shape, cuts, -0.22, 0.18) * entries
    return jnp.clip(entries, min=-limit, max=limit).astype(kind)


def heavy_noise(stream_key, shape, deviation, bound, cuts, heavy, kind=jnp.bfloat16):
    drawn = deviation * jax.random.normal(stream_key, shape, jnp.float32)
    if cuts:
        drawn = drawn * block_levels(stream_key, shape, cuts, -0.22, 0.18)
    return jnp.clip(spiked(drawn, jax.random.fold_in(stream_key, 3), *heavy), -bound, bound).astype(kind)


def setup_inputs(seed: int = 0) -> dict:
    keys = jax.random.split(jax.random.key(seed), 8)
    return {
        "tokens": draw_tokens(jax.random.fold_in(keys[7], 71), 0),
        "norm_gain": jnp.clip(1.0 + 0.1 * jax.random.normal(keys[1], (D,), jnp.float32), 0.5, 1.5),
        "w_query": draw_w_query(jax.random.fold_in(keys[7], 71), 0),
        "w_key": draw_w_key(jax.random.fold_in(keys[7], 71), 0),
        "w_value": normal_values(keys[4], (D, KD), D ** -0.5, 0.09375, ((1, 16),)),
        "w_output": normal_values(keys[5], (QD, D), QD ** -0.5, 0.09375, ((0, 16),)),
        "d_mixed": heavy_noise(keys[6], (TOKENS, D), 1.0, 24.0, ((0, 256),), (0, 1, 256, 6.0)),
    }


cap_value = 50.0

def norm_rows(tokens, norm_gain):
    values = tokens.astype(jnp.float32)
    scale = lax.rsqrt(lax.optimization_barrier(jnp.mean(values * values, axis=-1, keepdims=True)) + 1e-06)
    return (values * scale * norm_gain).astype(jnp.bfloat16)

def attend(query, key, value):
    length = query.shape[0]
    groups = key.shape[1] // HEAD
    ratio = query.shape[1] // key.shape[1]
    qf = query.astype(jnp.float32).reshape(length, groups, ratio, HEAD)
    kf = key.astype(jnp.float32).reshape(length, groups, HEAD)
    vf = value.astype(jnp.float32).reshape(length, groups, HEAD)
    scores = jnp.einsum('skgd,tkd->kgst', qf, kf) / math.sqrt(D // HEADS)
    capped = cap_value * jnp.tanh(scores / cap_value)
    row_pos = lax.broadcasted_iota(jnp.int32, (length, length), 0)
    col_pos = lax.broadcasted_iota(jnp.int32, (length, length), 1)
    visible = row_pos >= col_pos
    weights = jnp.where(visible, jnp.exp(capped), 0.0)
    log_total = jnp.log(lax.optimization_barrier(jnp.sum(weights, axis=-1, keepdims=True)))
    probs = jnp.exp(jnp.where(visible, capped - log_total, -1e+30)).astype(jnp.bfloat16)
    context = jnp.einsum('kgst,tkd->skgd', probs.astype(jnp.float32), vf)
    return context.reshape(length, groups * ratio * HEAD).astype(jnp.bfloat16)

def inner_rows(left, right):
    return lax.dot_general(left, right, (((0,), (0,)), ((), ())), preferred_element_type=jnp.float32)

def reference(tokens, norm_gain, w_query, w_key, w_value, w_output, d_mixed):
    normed = norm_rows(tokens, norm_gain)
    query = jnp.dot(normed, w_query, preferred_element_type=jnp.float32).astype(jnp.bfloat16)
    key = jnp.dot(normed, w_key, preferred_element_type=jnp.float32).astype(jnp.bfloat16)
    value = jnp.dot(normed, w_value, preferred_element_type=jnp.float32).astype(jnp.bfloat16)
    d_context = lax.dot_general(d_mixed, w_output, (((1,), (1,)), ((), ())), preferred_element_type=jnp.float32).astype(jnp.bfloat16)

    def one_sequence(pieces):
        qs, ks, vs, ds = pieces
        context, back = jax.vjp(attend, qs, ks, vs)
        dq, dk, dv = back(ds)
        return (context, dq, dk, dv)
    context, d_query, d_key, d_value = lax.map(one_sequence, (query.reshape(N_DP, SEQ, QD), key.reshape(N_DP, SEQ, KD), value.reshape(N_DP, SEQ, KD), d_context.reshape(N_DP, SEQ, QD)))
    context = context.reshape(TOKENS, QD)
    d_query = d_query.reshape(TOKENS, QD).astype(jnp.bfloat16)
    d_key = d_key.reshape(TOKENS, KD).astype(jnp.bfloat16)
    d_value = d_value.reshape(TOKENS, KD).astype(jnp.bfloat16)
    qcols = QD // N_TENSOR
    kcols = KD // N_TENSOR

    def add_output(total, index):
        start_q = (index * qcols).astype(jnp.int32)
        part_ctx = lax.dynamic_slice_in_dim(context, start_q, qcols, 1)
        part_w = lax.dynamic_slice_in_dim(w_output, start_q, qcols, 0)
        term = jnp.dot(part_ctx, part_w, preferred_element_type=jnp.float32).astype(jnp.bfloat16)
        return (total + term.astype(jnp.float32), None)
    summed, _ = lax.scan(add_output, jnp.zeros((TOKENS, D), jnp.float32), jnp.arange(N_TENSOR, dtype=jnp.int32))
    mixed = (tokens.astype(jnp.float32) + summed).astype(jnp.bfloat16)

    def add_input(total, index):
        start_q = (index * qcols).astype(jnp.int32)
        start_k = (index * kcols).astype(jnp.int32)
        dims = (((1,), (1,)), ((), ()))
        term = lax.dot_general(lax.dynamic_slice_in_dim(d_query, start_q, qcols, 1), lax.dynamic_slice_in_dim(w_query, start_q, qcols, 1), dims, preferred_element_type=jnp.float32)
        term = term + lax.dot_general(lax.dynamic_slice_in_dim(d_key, start_k, kcols, 1), lax.dynamic_slice_in_dim(w_key, start_k, kcols, 1), dims, preferred_element_type=jnp.float32)
        term = term + lax.dot_general(lax.dynamic_slice_in_dim(d_value, start_k, kcols, 1), lax.dynamic_slice_in_dim(w_value, start_k, kcols, 1), dims, preferred_element_type=jnp.float32)
        return (total + term.astype(jnp.bfloat16).astype(jnp.float32), None)
    d_normed, _ = lax.scan(add_input, jnp.zeros((TOKENS, D), jnp.float32), jnp.arange(N_TENSOR, dtype=jnp.int32))
    values = tokens.astype(jnp.float32)
    scale = lax.rsqrt(lax.optimization_barrier(jnp.mean(values * values, axis=-1, keepdims=True)) + 1e-06)
    upstream = norm_gain * d_normed
    back_norm = scale * upstream - values * scale ** 3 * lax.optimization_barrier(jnp.mean(upstream * values, axis=-1, keepdims=True))
    d_tokens = (d_mixed.astype(jnp.float32) + back_norm).astype(jnp.bfloat16)
    dw_query = inner_rows(normed, d_query)
    dw_key = inner_rows(normed, d_key)
    dw_value = inner_rows(normed, d_value)
    dw_output = inner_rows(context, d_mixed)
    return (mixed, d_tokens, dw_query, dw_key, dw_value, dw_output)
```

```python
import functools
import math

import jax
import jax.numpy as jnp
from jax import lax
from jax.experimental import pallas as pl
from jax.experimental.pallas import tpu as pltpu
from jax.sharding import PartitionSpec as P

D = 4608
HEADS = 32
HEAD = 128
SEQ = 512
ROWS = 32
QC = 256
CAP = 50.0
SCALE = 1.0 / math.sqrt(D // HEADS)
CHUNK = D // 8
HALF = D // 16
TILE = 512
MESH = pl.DeviceIdType.MESH
BF = jnp.bfloat16
F32 = jnp.float32

AB = (((1,), (0,)), ((), ()))
ABT = (((1,), (1,)), ((), ()))
ATB = (((0,), (0,)), ((), ()))


def dot(a, b, dims=AB):
    return lax.dot_general(a, b, dims, preferred_element_type=F32)


def at(i, n):
    return pl.ds(pl.multiple_of(i * n, n), n)


def kernel(
    tok, gain, wq, wk, wv, wo, dm,
    mixed_o, dtok_o, dwq_o, dwk_o, dwv_o, dwo_o,
    fn, fd, w, wout, qkv, ctx, dctx, dqkv, acc, probs, slope,
    grad, recv1, recv, recv_y, part, sib_in, far_in,
    w_sem, ag_s, ag_r, z_s, z_r, y_s, y_r, sib_s, sib_r, far_s, far_r,
):
    dp, tensor = lax.axis_index("dp"), lax.axis_index("tensor")
    z, yh = lax.div(dp, 2), lax.rem(dp, 2)
    yl, x, c = lax.div(tensor, 8), lax.rem(lax.div(tensor, 2), 4), lax.rem(tensor, 2)
    chip = yl * 4 + x

    def device(z_, yh_, yl_, x_, c_):
        return (z_ * 2 + yh_, yl_ * 8 + x_ * 2 + c_)

    def ring(i, step, n):
        return lax.rem(i + step + n, n)

    right = device(z, yh, yl, ring(x, 1, 4), c)
    left = device(z, yh, yl, ring(x, -1, 4), c)
    across = device(z, yh, 1 - yl, x, c)
    sibling = device(z, yh, yl, x, 1 - c)
    up = device(ring(z, 1, 8), yh, yl, x, c)
    down = device(ring(z, -1, 8), yh, yl, x, c)
    other_y = device(z, 1 - yh, yl, x, c)

    def chip_at(j):
        k = lax.rem(chip + j, 8)
        return k, device(z, yh, lax.div(k, 4), lax.rem(k, 4), c)

    weight_in = [
        pltpu.make_async_copy(wq, w.at[:, pl.ds(0, 256)], w_sem.at[0]),
        pltpu.make_async_copy(wk, w.at[:, pl.ds(256, 128)], w_sem.at[1]),
        pltpu.make_async_copy(wv, w.at[:, pl.ds(384, 128)], w_sem.at[2]),
        pltpu.make_async_copy(wo, wout, w_sem.at[3]),
    ]
    for copy in weight_in:
        copy.start()

    barrier = pltpu.get_barrier_semaphore()
    peers = [sibling, up, down, other_y] + [chip_at(j)[1] for j in range(1, 8)]
    for peer in peers:
        pl.semaphore_signal(barrier, inc=1, device_id=peer, device_id_type=MESH)

    values = tok[...].astype(F32)
    scale = lax.rsqrt(jnp.mean(values * values, axis=-1, keepdims=True) + 1e-06)
    mine = at(tensor, ROWS)
    fn[mine, :] = (values * scale * gain[...]).astype(BF)
    fd[mine, :] = dm[...]
    pl.semaphore_wait(barrier, len(peers))

    def block(dx, dy, core):
        return (yl if dy == 0 else 1 - yl) * 8 + ring(x, dx, 4) * 2 + core

    def gather(full, a):
        def copy(i, rows, to):
            return pltpu.make_async_remote_copy(
                src_ref=full.at[rows, :], dst_ref=full.at[rows, :],
                send_sem=ag_s.at[a, i], recv_sem=ag_r.at[a, i],
                device_id=to, device_id_type=MESH,
            )

        def whole(dx, dy, core=c):
            return at(block(dx, dy, core), ROWS)

        def first(dx):
            return at(block(dx, 0, c) * 2, ROWS // 2)

        def second(dx):
            return at(block(dx, 0, c) * 2 + 1, ROWS // 2)

        order = [(0, 0), (-1, 0), (1, 0), (0, 1), (2, 0), (-1, 1), (1, 1), (2, 1)]

        def to_sibling(i):
            copy(8 + i, whole(*order[i]), sibling).start()

        def step1():
            copy(2, whole(0, 0), across).start()
            copy(0, whole(0, 0), right).start()
            copy(1, whole(0, 0), left).start()
            to_sibling(0)

        def step2():
            copy(0, whole(-1, 0), right).wait_recv()
            copy(3, first(-1), right).start()
            copy(1, whole(1, 0), left).wait_recv()
            copy(4, second(1), left).start()
            copy(2, whole(0, 1), across).wait_recv()
            copy(5, whole(0, 1), right).start()
            copy(6, whole(0, 1), left).start()
            for i in (1, 2, 3):
                to_sibling(i)

        def step3():
            copy(3, first(2), right).wait_recv()
            copy(4, second(2), left).wait_recv()
            copy(7, whole(2, 0), across).start()
            to_sibling(4)

        def step4():
            copy(5, whole(-1, 1), right).wait_recv()
            to_sibling(5)
            copy(6, whole(1, 1), left).wait_recv()
            to_sibling(6)
            copy(7, whole(2, 1), across).wait_recv()
            to_sibling(7)

        def finish():
            for i in range(8):
                copy(8 + i, whole(*order[i], 1 - c), sibling).wait_recv()

        def sent():
            for i, to in ((0, right), (1, left), (2, across), (5, right), (6, left), (7, across)):
                copy(i, whole(0, 0), to).wait_send()
            copy(3, first(0), right).wait_send()
            copy(4, second(0), left).wait_send()
            for i in range(8):
                copy(8 + i, whole(0, 0), sibling).wait_send()

        return step1, step2, step3, step4, finish, sent

    n1, n2, n3, n4, n_end, n_sent = gather(fn, 0)
    d1, d2, d3, d4, d_end, d_sent = gather(fd, 1)
    n1()
    n2()
    d1()
    n3()
    n4()
    n_end()

    for copy in weight_in[:3]:
        copy.wait()
    acc[...] = jnp.zeros_like(acc)

    def project(i, carry):
        acc[...] += dot(fn[:, at(i, TILE)], w[at(i, TILE), :])
        return carry

    lax.fori_loop(0, D // TILE, project, 0)
    qkv[...] = acc[...].astype(BF)

    d2()

    blocks = ((0, 256), (256, 512))
    for h in range(2):
        for lo, hi in blocks:
            q = qkv[lo:hi, h * HEAD : (h + 1) * HEAD]
            scores = dot(q, qkv[:hi, 256:384], ABT)
            th = jnp.tanh(scores * (SCALE / CAP))
            row = lax.broadcasted_iota(jnp.int32, (256, hi), 0) + lo
            col = lax.broadcasted_iota(jnp.int32, (256, hi), 1)
            weight = jnp.where(row >= col, jnp.exp(CAP * th), 0.0)
            p = weight * (1.0 / jnp.sum(weight, axis=-1, keepdims=True))
            probs[h, lo:hi, :hi] = p
            slope[h, lo:hi, :hi] = p * ((1.0 - th * th) * SCALE)
            ctx[lo:hi, h * HEAD : (h + 1) * HEAD] = dot(
                p.astype(BF), qkv[:hi, 384:512]
            ).astype(BF)

    d3()

    def scatter(a):
        def sib_copy():
            return pltpu.make_async_remote_copy(
                src_ref=part.at[a, :, 1 - c], dst_ref=sib_in.at[a],
                send_sem=sib_s.at[a], recv_sem=sib_r.at[a],
                device_id=sibling, device_id_type=MESH,
            )

        def far_copy(j):
            k, to = chip_at(j)
            return pltpu.make_async_remote_copy(
                src_ref=part.at[a, k, c], dst_ref=far_in.at[a, j - 1],
                send_sem=far_s.at[a, j - 1], recv_sem=far_r.at[a, j - 1],
                device_id=to, device_id_type=MESH,
            )

        def start():
            sib_copy().start()

        def spread():
            sib_copy().wait()

            def one(k, carry):
                part[a, k, c] = (
                    part[a, k, c].astype(F32) + sib_in[a, k].astype(F32)
                ).astype(BF)
                return carry

            lax.fori_loop(0, 8, one, 0)
            for j in range(1, 8):
                far_copy(j).start()

        def total():
            for j in range(1, 8):
                far_copy(j).wait_recv()
            out = part[a, chip, c].astype(F32)
            for j in range(7):
                out = out + far_in[a, j].astype(F32)
            return out

        def sent():
            for j in range(1, 8):
                far_copy(j).wait_send()

        return start, spread, total, sent

    m_start, m_spread, m_total, m_sent = scatter(0)
    g_start, g_spread, g_total, g_sent = scatter(1)

    weight_in[3].wait()

    def mix(i, carry):
        term = dot(ctx[...], wout[:, at(i, TILE)])
        part[0, :, :, :, at(i, TILE)] = term.astype(BF).reshape(8, 2, ROWS, TILE)
        return carry

    lax.fori_loop(0, D // TILE, mix, 0)
    m_start()
    d4()
    d_end()

    acc[:, :QC] = jnp.zeros((SEQ, QC), F32)

    def back_out(i, carry):
        acc[:, :QC] += dot(fd[:, at(i, TILE)], wout[:, at(i, TILE)], ABT)
        return carry

    lax.fori_loop(0, D // TILE, back_out, 0)
    dctx[...] = acc[:, :QC].astype(BF)

    def z_chunk(k):
        return at(ring(z, k, 8), CHUNK)

    def z_half(k, b):
        return at(ring(z, k, 8) * 2 + b, HALF)

    def z_steps(p):
        def first_copy(way):
            return pltpu.make_async_remote_copy(
                src_ref=grad.at[p, z_half(4, way), :], dst_ref=recv1.at[p, way],
                send_sem=z_s.at[p, 0, way], recv_sem=z_r.at[p, 0, way],
                device_id=(up, down)[way], device_id_type=MESH,
            )

        def later_copy(s, way):
            return pltpu.make_async_remote_copy(
                src_ref=grad.at[p, z_chunk((4 - s) * (1 - 2 * way)), :],
                dst_ref=recv.at[p, s - 1, way],
                send_sem=z_s.at[p, s, way], recv_sem=z_r.at[p, s, way],
                device_id=(up, down)[way], device_id_type=MESH,
            )

        def y_copy():
            return pltpu.make_async_remote_copy(
                src_ref=grad.at[p, z_half(0, 1 - yh), :], dst_ref=recv_y.at[p],
                send_sem=y_s.at[p], recv_sem=y_r.at[p],
                device_id=other_y, device_id_type=MESH,
            )

        def start():
            for way in range(2):
                first_copy(way).start()

        def step(s):
            for way in range(2):
                if s == 1:
                    first_copy(way).wait_recv()
                    rows, arrived = z_half(3 * (1 - 2 * way), way), recv1[p, way]
                else:
                    later_copy(s - 1, way).wait_recv()
                    rows, arrived = z_chunk((4 - s) * (1 - 2 * way)), recv[p, s - 2, way]
                grad[p, rows, :] = (
                    grad[p, rows, :].astype(F32) + arrived.astype(F32)
                ).astype(BF)
                later_copy(s, way).start()

        def end():
            later_copy(3, 0).wait_recv()
            later_copy(3, 1).wait_recv()
            rows = z_chunk(0)
            grad[p, rows, :] = (
                grad[p, rows, :].astype(F32)
                + recv[p, 2, 0].astype(F32)
                + recv[p, 2, 1].astype(F32)
            ).astype(BF)
            y_copy().start()

        def total():
            y_copy().wait()
            return grad[p, z_half(0, yh), :].astype(F32) + recv_y[p].astype(F32)

        def sent():
            for way in range(2):
                first_copy(way).wait_send()
                for s in range(1, 4):
                    later_copy(s, way).wait_send()

        return start, step, end, total, sent

    o_start, o_step, o_end, o_total, o_sent = z_steps(0)
    q_start, q_step, q_end, q_total, q_sent = z_steps(1)
    k_start, k_step, k_end, k_total, k_sent = z_steps(2)

    def grad_out(i, carry):
        term = dot(fd[:, at(i, 256)], ctx[...], ATB)
        grad[0, at(i, 256), :] = term.astype(BF)
        return carry

    lax.fori_loop(0, D // 256, grad_out, 0)
    o_start()
    m_spread()

    acc[...] = jnp.zeros_like(acc)
    for h in range(2):
        for lo, hi in blocks:
            heads = slice(h * HEAD, (h + 1) * HEAD)
            d_ctx = dctx[lo:hi, heads]
            p = probs[h, lo:hi, :hi]
            d_p = dot(d_ctx, qkv[:hi, 384:512], ABT)
            inner = jnp.sum(p * d_p, axis=-1, keepdims=True)
            d_s = (slope[h, lo:hi, :hi] * (d_p - inner)).astype(BF)
            dqkv[lo:hi, heads] = dot(d_s, qkv[:hi, 256:384]).astype(BF)
            acc[:hi, 256:384] += dot(d_s, qkv[lo:hi, heads], ATB)
            acc[:hi, 384:512] += dot(p.astype(BF), d_ctx, ATB)
    dqkv[:, 256:512] = acc[:, 256:512].astype(BF)

    o_step(1)

    def grad_in(i, carry):
        term = dot(fn[:, at(i, 256)], dqkv[...], ATB).astype(BF)
        grad[1, at(i, 256), :] = term[:, :256]
        grad[2, at(i, 256), :] = term[:, 256:]
        return carry

    lax.fori_loop(0, D // 256, grad_in, 0)
    q_start()
    k_start()
    o_step(2)

    def back_in(i, carry):
        term = dot(dqkv[...], w[at(i, TILE), :], ABT)
        part[1, :, :, :, at(i, TILE)] = term.astype(BF).reshape(8, 2, ROWS, TILE)
        return carry

    lax.fori_loop(0, D // TILE, back_in, 0)
    g_start()
    q_step(1)
    k_step(1)
    o_step(3)
    g_spread()
    q_step(2)
    k_step(2)
    mixed_o[...] = (tok[...].astype(F32) + m_total()).astype(BF)
    o_end()
    q_step(3)
    k_step(3)

    d_normed = g_total()
    upstream = gain[...] * d_normed
    values = tok[...].astype(F32)
    scale = lax.rsqrt(jnp.mean(values * values, axis=-1, keepdims=True) + 1e-06)
    back_norm = scale * upstream - values * (scale * scale * scale) * jnp.mean(
        upstream * values, axis=-1, keepdims=True
    )
    dtok_o[...] = (dm[...].astype(F32) + back_norm).astype(BF)
    dwo_o[...] = o_total()

    q_end()
    k_end()
    dwq_o[...] = q_total()
    d_kv = k_total()
    dwk_o[...] = d_kv[:, :HEAD]
    dwv_o[...] = d_kv[:, HEAD:]

    for done in (n_sent, d_sent, m_sent, g_sent, o_sent, q_sent, k_sent):
        done()


def on_device(tokens, norm_gain, w_query, w_key, w_value, w_output, d_mixed):
    vmem = pl.BlockSpec(memory_space=pltpu.VMEM)
    hbm = pl.BlockSpec(memory_space=pl.ANY)
    dma = pltpu.SemaphoreType.DMA
    mixed, d_tokens, dw_query, dw_key, dw_value, dw_out_t = pl.pallas_call(
        kernel,
        out_shape=(
            jax.ShapeDtypeStruct((ROWS, D), BF),
            jax.ShapeDtypeStruct((ROWS, D), BF),
            jax.ShapeDtypeStruct((HALF, QC), F32),
            jax.ShapeDtypeStruct((HALF, HEAD), F32),
            jax.ShapeDtypeStruct((HALF, HEAD), F32),
            jax.ShapeDtypeStruct((HALF, QC), F32),
        ),
        in_specs=[vmem, vmem, hbm, hbm, hbm, hbm, vmem],
        out_specs=(vmem,) * 6,
        scratch_shapes=[
            pltpu.VMEM((SEQ, D), BF),
            pltpu.VMEM((SEQ, D), BF),
            pltpu.VMEM((D, 512), BF),
            pltpu.VMEM((QC, D), BF),
            pltpu.VMEM((SEQ, 512), BF),
            pltpu.VMEM((SEQ, QC), BF),
            pltpu.VMEM((SEQ, QC), BF),
            pltpu.VMEM((SEQ, 512), BF),
            pltpu.VMEM((SEQ, 512), F32),
            pltpu.VMEM((2, SEQ, SEQ), F32),
            pltpu.VMEM((2, SEQ, SEQ), F32),
            pltpu.VMEM((3, D, QC), BF),
            pltpu.VMEM((3, 2, HALF, QC), BF),
            pltpu.VMEM((3, 3, 2, CHUNK, QC), BF),
            pltpu.VMEM((3, HALF, QC), BF),
            pltpu.VMEM((2, 8, 2, ROWS, D), BF),
            pltpu.VMEM((2, 8, ROWS, D), BF),
            pltpu.VMEM((2, 7, ROWS, D), BF),
            dma((4,)),
            dma((2, 16)),
            dma((2, 16)),
            dma((3, 4, 2)),
            dma((3, 4, 2)),
            dma((3,)),
            dma((3,)),
            dma((2,)),
            dma((2,)),
            dma((2, 7)),
            dma((2, 7)),
        ],
        compiler_params=pltpu.CompilerParams(
            collective_id=0, has_side_effects=True, vmem_limit_bytes=64 * 2**20 - 2**17
        ),
        cost_estimate=pl.CostEstimate(
            flops=12 * 10**9, bytes_accessed=10**7, transcendentals=10**6
        ),
    )(tokens, norm_gain.reshape(1, D), w_query, w_key, w_value, w_output, d_mixed)
    return (mixed, d_tokens, dw_query, dw_key, dw_value, dw_out_t.T)


def solution(mesh):
    return jax.shard_map(
        on_device,
        mesh=mesh,
        in_specs=(
            P(("dp", "tensor"), None),
            P(),
            P(None, "tensor"),
            P(None, "tensor"),
            P(None, "tensor"),
            P("tensor", None),
            P(("dp", "tensor"), None),
        ),
        out_specs=(
            P(("dp", "tensor"), None),
            P(("dp", "tensor"), None),
            P("dp", "tensor"),
            P("dp", "tensor"),
            P("dp", "tensor"),
            P("tensor", "dp"),
        ),
        check_vma=False,
    )
```

```python
import functools
import math

import jax
import jax.numpy as jnp
from jax import lax
from jax.experimental import pallas as pl
from jax.experimental.pallas import tpu as pltpu
from jax.sharding import PartitionSpec as P

D = 4608
HEADS = 32
HEAD = 128
SEQ = 512
ROWS = 32
QC = 256
CAP = 50.0
SCALE = 1.0 / math.sqrt(D // HEADS)
SIDE = D // 2
HALF = D // 16
TILE = 512
MESH = pl.DeviceIdType.MESH
BF = jnp.bfloat16
F32 = jnp.float32

AB = (((1,), (0,)), ((), ()))
ABT = (((1,), (1,)), ((), ()))
ATB = (((0,), (0,)), ((), ()))


def dot(a, b, dims=AB):
    return lax.dot_general(a, b, dims, preferred_element_type=F32)


def at(i, n):
    return pl.ds(pl.multiple_of(i * n, n), n)


def kernel(
    tok, gain, wq, wk, wv, wo, dm,
    mixed_o, dtok_o, dwq_o, dwk_o, dwv_o, dwo_o,
    fn, fd, fx, w, wout, qkv, ctx, dctx, dqkv, dqkv_x, acc, probs, slope,
    grad_o, grad_i, recv_o, recv_i, recv_y, part, sib_in, far_in,
    w_sem, ag_s, ag_r, zo_s, zo_r, zi_s, zi_r, y_s, y_r, sib_s, sib_r, far_s, far_r,
):
    dp, tensor = lax.axis_index("dp"), lax.axis_index("tensor")
    z, yh = lax.div(dp, 2), lax.rem(dp, 2)
    yl, x, c = lax.div(tensor, 8), lax.rem(lax.div(tensor, 2), 4), lax.rem(tensor, 2)

    def device(z_, yh_, yl_, x_, c_):
        return (z_ * 2 + yh_, yl_ * 8 + x_ * 2 + c_)

    def ring(i, step, n):
        return lax.rem(i + step + n, n)

    right = device(z, yh, yl, ring(x, 1, 4), c)
    left = device(z, yh, yl, ring(x, -1, 4), c)
    across = device(z, yh, 1 - yl, x, c)
    sibling = device(z, yh, yl, x, 1 - c)
    up = device(ring(z, 1, 8), yh, yl, x, c)
    down = device(ring(z, -1, 8), yh, yl, x, c)
    other_y = device(z, 1 - yh, yl, x, c)

    def remote(src, dst, send_sem, recv_sem, to):
        return pltpu.make_async_remote_copy(
            src_ref=src, dst_ref=dst, send_sem=send_sem, recv_sem=recv_sem,
            device_id=to, device_id_type=MESH,
        )

    columns = (pl.ds(0, 256), pl.ds(256, 128), pl.ds(384, 128))
    for i, weight in enumerate((wq, wk, wv)):
        for h in range(2):
            for k in range(8):
                pltpu.make_async_copy(
                    weight.at[pl.ds((2 * k + h) * HALF, HALF), :],
                    w.at[pl.ds((8 * h + k) * HALF, HALF), columns[i]],
                    w_sem.at[i],
                ).start()
    wout_in = pltpu.make_async_copy(wo, wout, w_sem.at[3])
    wout_in.start()

    barrier = pltpu.get_barrier_semaphore()
    peers = (sibling, left, right, across, up, down, other_y)
    for peer in peers:
        pl.semaphore_signal(barrier, inc=1, device_id=peer, device_id_type=MESH)

    values = tok[...].astype(F32)
    scale = lax.rsqrt(jnp.mean(values * values, axis=-1, keepdims=True) + 1e-06)
    normed = values * scale * gain[...]
    mine = at(tensor, ROWS)
    fn[mine, :] = jnp.concatenate(
        [
            normed[:, (2 * k + h) * HALF : (2 * k + h + 1) * HALF]
            for h in range(2)
            for k in range(8)
        ],
        axis=1,
    ).astype(BF)
    fd[mine, :] = dm[...]
    pl.semaphore_wait(barrier, len(peers))

    def block(dx, dy, core):
        return (yl if dy == 0 else 1 - yl) * 8 + ring(x, dx, 4) * 2 + core

    def gather(full, a):
        def copy(i, rows, to):
            return remote(
                full.at[rows, :], full.at[rows, :], ag_s.at[a, i], ag_r.at[a, i], to
            )

        def whole(dx, dy, core=c):
            return at(block(dx, dy, core), ROWS)

        def first(dx):
            return at(block(dx, 0, c) * 2, ROWS // 2)

        def second(dx):
            return at(block(dx, 0, c) * 2 + 1, ROWS // 2)

        order = [(0, 0), (-1, 0), (1, 0), (0, 1), (2, 0), (-1, 1), (1, 1), (2, 1)]

        def to_sibling(i):
            copy(8 + i, whole(*order[i]), sibling).start()

        def step1x():
            copy(0, whole(0, 0), right).start()
            copy(1, whole(0, 0), left).start()
            to_sibling(0)

        def step1y():
            copy(2, whole(0, 0), across).start()

        def step2():
            copy(0, whole(-1, 0), right).wait_recv()
            copy(3, first(-1), right).start()
            copy(1, whole(1, 0), left).wait_recv()
            copy(4, second(1), left).start()
            copy(2, whole(0, 1), across).wait_recv()
            copy(5, whole(0, 1), right).start()
            copy(6, whole(0, 1), left).start()
            for i in (1, 2, 3):
                to_sibling(i)

        def step3():
            copy(3, first(2), right).wait_recv()
            copy(4, second(2), left).wait_recv()
            copy(7, whole(2, 0), across).start()
            to_sibling(4)

        def step4():
            copy(5, whole(-1, 1), right).wait_recv()
            to_sibling(5)
            copy(6, whole(1, 1), left).wait_recv()
            to_sibling(6)
            copy(7, whole(2, 1), across).wait_recv()
            to_sibling(7)

        def finish():
            for i in range(8):
                copy(8 + i, whole(*order[i], 1 - c), sibling).wait_recv()

        def sent():
            for i, to in ((0, right), (1, left), (2, across), (5, right), (6, left), (7, across)):
                copy(i, whole(0, 0), to).wait_send()
            copy(3, first(0), right).wait_send()
            copy(4, second(0), left).wait_send()
            for i in range(8):
                copy(8 + i, whole(0, 0), sibling).wait_send()

        return step1x, step1y, step2, step3, step4, finish, sent

    n1x, n1y, n2, n3, n4, n_end, n_sent = gather(fn, 0)
    d1x, d1y, d2, d3, d4, d_end, d_sent = gather(fd, 1)
    x1x, x1y, x2, x3, x4, x_end, x_sent = gather(fx, 2)

    def side(h):
        return pl.ds(pl.multiple_of(h * SIDE, SIDE), SIDE)

    pair_rows = remote(
        fn.at[mine, side(1 - yh)], fx.at[mine, :], y_s.at[1], y_r.at[1], other_y
    )

    n1x()
    n1y()
    n2()
    d1x()
    pair_rows.start()
    n3()
    d1y()
    n4()
    n_end()

    for i, weight in enumerate((wq, wk, wv)):
        pltpu.make_async_copy(weight, w.at[:, columns[i]], w_sem.at[i]).wait()
    acc[...] = jnp.zeros_like(acc)

    def project(i, carry):
        acc[...] += dot(fn[:, at(i, TILE)], w[at(i, TILE), :])
        return carry

    lax.fori_loop(0, 5, project, 0)
    d2()
    lax.fori_loop(5, 9, project, 0)
    qkv[...] = acc[...].astype(BF)
    d3()
    pair_rows.wait_recv()
    x1x()
    x1y()

    blocks = ((0, 256), (256, 512))
    for h in range(2):
        for lo, hi in blocks:
            q = qkv[lo:hi, h * HEAD : (h + 1) * HEAD]
            scores = dot(q, qkv[:hi, 256:384], ABT)
            th = jnp.tanh(scores * (SCALE / CAP))
            row = lax.broadcasted_iota(jnp.int32, (256, hi), 0) + lo
            col = lax.broadcasted_iota(jnp.int32, (256, hi), 1)
            weight = jnp.where(row >= col, jnp.exp(CAP * th), 0.0)
            p = weight * (1.0 / jnp.sum(weight, axis=-1, keepdims=True))
            probs[h, lo:hi, :hi] = p
            slope[h, lo:hi, :hi] = p * ((1.0 - th * th) * SCALE)
            ctx[lo:hi, h * HEAD : (h + 1) * HEAD] = dot(
                p.astype(BF), qkv[:hi, 384:512]
            ).astype(BF)

    def scatter(a):
        def chip(dx, dy):
            return (yl if dy == 0 else 1 - yl) * 4 + ring(x, dx, 4)

        top, low = slice(0, ROWS // 2), slice(ROWS // 2, ROWS)

        def sib_copy():
            return remote(
                part.at[a, :, 1 - c], sib_in.at[a], sib_s.at[a], sib_r.at[a], sibling
            )

        def copy(i):
            dx, dy, slot, rows, to = (
                (2, 1, 0, None, across),
                (1, 1, 1, None, right),
                (-1, 1, 2, None, left),
                (2, 0, 3, top, right),
                (2, 0, 3, low, left),
                (1, 0, 4, None, right),
                (-1, 0, 5, None, left),
                (0, 1, 6, None, across),
            )[i]
            src, dst = part.at[a, chip(dx, dy), c], far_in.at[a, slot]
            if rows is not None:
                src, dst = src.at[rows], dst.at[rows]
            return remote(src, dst, far_s.at[a, i], far_r.at[a, i], to)

        def add(dx, dy, slots, rows=slice(0, ROWS)):
            k = chip(dx, dy)
            total = part[a, k, c, rows].astype(F32)
            for slot in slots:
                total = total + far_in[a, slot, rows].astype(F32)
            part[a, k, c, rows] = total.astype(BF)

        def start():
            sib_copy().start()

        def spread():
            sib_copy().wait()

            def one(k, carry):
                part[a, k, c] = (
                    part[a, k, c].astype(F32) + sib_in[a, k].astype(F32)
                ).astype(BF)
                return carry

            lax.fori_loop(0, 8, one, 0)
            for i in range(3):
                copy(i).start()

        def middle():
            copy(0).wait_recv()
            add(2, 0, (0,))
            copy(3).start()
            copy(4).start()
            copy(1).wait_recv()
            copy(2).wait_recv()
            add(0, 1, (1, 2))
            copy(7).start()

        def late():
            copy(3).wait_recv()
            add(1, 0, (3,), top)
            copy(5).start()
            copy(4).wait_recv()
            add(-1, 0, (3,), low)
            copy(6).start()

        def total():
            out = part[a, chip(0, 0), c].astype(F32)
            for i, slot in ((5, 4), (6, 5), (7, 6)):
                copy(i).wait_recv()
                out = out + far_in[a, slot].astype(F32)
            return out

        def sent():
            for i in range(8):
                copy(i).wait_send()

        return start, spread, middle, late, total, sent

    m_start, m_spread, m_middle, m_late, m_total, m_sent = scatter(0)
    g_start, g_spread, g_middle, g_late, g_total, g_sent = scatter(1)

    wout_in.wait()

    def mix(i, carry):
        term = dot(ctx[...], wout[:, at(i, TILE)])
        part[0, :, :, :, at(i, TILE)] = term.astype(BF).reshape(8, 2, ROWS, TILE)
        return carry

    lax.fori_loop(0, D // TILE, mix, 0)
    m_start()
    d4()
    x2()
    d_end()

    away = (4, 3, 3, 2, 2, 1, 1)

    def z_steps(grad, recv, send_sem, recv_sem, rows):
        half = rows // 2

        def place(i, way, distance):
            part_of = way if i % 2 == 0 else 1 - way
            return at(ring(z, distance * (1 - 2 * way), 8) * 2 + part_of, half)

        def copy(i, way):
            return remote(
                grad.at[place(i, way, away[i]), :], recv.at[i, way],
                send_sem.at[i, way], recv_sem.at[i, way], (up, down)[way],
            )

        def arrive(i, way):
            copy(i, way).wait_recv()
            here = place(i, way, away[i] - 1)
            grad[here, :] = (
                grad[here, :].astype(F32) + recv[i, way].astype(F32)
            ).astype(BF)

        def start():
            for i in range(2):
                for way in range(2):
                    copy(i, way).start()

        def step(i):
            for way in range(2):
                arrive(i - 2, way)
                copy(i, way).start()

        def end():
            for i in (5, 6):
                for way in range(2):
                    arrive(i, way)

        def sent():
            for i in range(7):
                for way in range(2):
                    copy(i, way).wait_send()

        return start, step, end, sent

    o_start, o_step, o_end, o_sent = z_steps(grad_o, recv_o, zo_s, zo_r, 2 * HALF)
    q_start, q_step, q_end, q_sent = z_steps(
        grad_i.at[0], recv_i.at[0], zi_s.at[0], zi_r.at[0], HALF
    )
    k_start, k_step, k_end, k_sent = z_steps(
        grad_i.at[1], recv_i.at[1], zi_s.at[1], zi_r.at[1], HALF
    )

    def grad_out(i, carry):
        term = dot(fd[:, at(i, 256)], ctx[...], ATB)
        grad_o[at(i, 256), :] = term.astype(BF)
        return carry

    lax.fori_loop(0, D // 256, grad_out, 0)
    o_start()

    acc[:, :QC] = jnp.zeros((SEQ, QC), F32)

    def back_out(i, carry):
        acc[:, :QC] += dot(fd[:, at(i, TILE)], wout[:, at(i, TILE)], ABT)
        return carry

    lax.fori_loop(0, D // TILE, back_out, 0)
    dctx[...] = acc[:, :QC].astype(BF)
    x3()
    m_spread()
    o_step(2)

    def pair_copy(i):
        cols = (pl.ds(0, 128), pl.ds(128, 128), pl.ds(256, 256))[i]
        return remote(
            dqkv.at[:, cols], dqkv_x.at[:, cols], y_s.at[2 + i], y_r.at[2 + i], other_y
        )

    acc[...] = jnp.zeros_like(acc)
    for h in range(2):
        for lo, hi in blocks:
            heads = slice(h * HEAD, (h + 1) * HEAD)
            d_ctx = dctx[lo:hi, heads]
            p = probs[h, lo:hi, :hi]
            d_p = dot(d_ctx, qkv[:hi, 384:512], ABT)
            inner = jnp.sum(p * d_p, axis=-1, keepdims=True)
            d_s = (slope[h, lo:hi, :hi] * (d_p - inner)).astype(BF)
            dqkv[lo:hi, heads] = dot(d_s, qkv[:hi, 256:384]).astype(BF)
            acc[:hi, 256:384] += dot(d_s, qkv[lo:hi, heads], ATB)
            acc[:hi, 384:512] += dot(p.astype(BF), d_ctx, ATB)
        pair_copy(h).start()
        if h == 0:
            x4()
            o_step(3)
    dqkv[:, 256:512] = acc[:, 256:512].astype(BF)
    pair_copy(2).start()
    o_step(4)
    m_middle()

    def back_in(i, carry):
        term = dot(dqkv[...], w[at(i, TILE), :], ABT)
        part[1, :, :, :, at(i, TILE)] = term.astype(BF).reshape(8, 2, ROWS, TILE)
        return carry

    lax.fori_loop(0, D // TILE, back_in, 0)
    g_start()
    o_step(5)
    m_late()
    g_spread()
    o_step(6)
    x_end()
    for i in range(3):
        pair_copy(i).wait_recv()

    def grad_in(i, carry):
        own = pl.ds(pl.multiple_of(yh * SIDE + i * 256, 256), 256)
        term = dot(fn[:, own], dqkv[...], ATB) + dot(fx[:, at(i, 256)], dqkv_x[...], ATB)
        term = term.astype(BF)
        grad_i[0, at(i, 256), :] = term[:, :256]
        grad_i[1, at(i, 256), :] = term[:, 256:]
        return carry

    lax.fori_loop(0, SIDE // 256, grad_in, 0)
    q_start()
    k_start()

    def keep(h):
        return at(z * 2 + h, HALF)

    o_end()
    y_copy = remote(grad_o.at[keep(1 - yh), :], recv_y, y_s.at[0], y_r.at[0], other_y)
    y_copy.start()
    q_step(2)
    k_step(2)
    g_middle()
    q_step(3)
    k_step(3)
    mixed_o[...] = (tok[...].astype(F32) + m_total()).astype(BF)
    q_step(4)
    k_step(4)
    g_late()
    q_step(5)
    k_step(5)
    y_copy.wait_recv()
    dwo_o[...] = grad_o[keep(yh), :].astype(F32) + recv_y[...].astype(F32)
    q_step(6)
    k_step(6)

    summed = g_total()
    d_normed = jnp.concatenate(
        [
            summed[:, (8 * h + k) * HALF : (8 * h + k + 1) * HALF]
            for k in range(8)
            for h in range(2)
        ],
        axis=1,
    )
    upstream = gain[...] * d_normed
    values = tok[...].astype(F32)
    scale = lax.rsqrt(jnp.mean(values * values, axis=-1, keepdims=True) + 1e-06)
    back_norm = scale * upstream - values * (scale * scale * scale) * jnp.mean(
        upstream * values, axis=-1, keepdims=True
    )
    dtok_o[...] = (dm[...].astype(F32) + back_norm).astype(BF)

    q_end()
    k_end()
    dwq_o[...] = grad_i[0, at(z, HALF), :].astype(F32)
    dwk_o[...] = grad_i[1, at(z, HALF), :HEAD].astype(F32)
    dwv_o[...] = grad_i[1, at(z, HALF), HEAD:].astype(F32)

    for done in (n_sent, d_sent, x_sent, m_sent, g_sent, o_sent, q_sent, k_sent):
        done()
    pair_rows.wait_send()
    y_copy.wait_send()
    for i in range(3):
        pair_copy(i).wait_send()


def hand_out(*refs):
    sources, results, held, sem = refs[:6], refs[6:12], refs[12:18], refs[18]
    loads = [
        pltpu.make_async_copy(source, ref, sem.at[0, i])
        for i, (source, ref) in enumerate(zip(sources, held))
    ]
    stores = [
        pltpu.make_async_copy(ref, result, sem.at[1, i])
        for i, (ref, result) in enumerate(zip(held, results))
    ]
    for load in loads:
        load.start()
    for load, store in zip(loads, stores):
        load.wait()
        store.start()
    for store in stores:
        store.wait()


def on_device(tokens, norm_gain, w_query, w_key, w_value, w_output, d_mixed):
    vmem = pl.BlockSpec(memory_space=pltpu.VMEM)
    hbm = pl.BlockSpec(memory_space=pl.ANY)
    dma = pltpu.SemaphoreType.DMA
    results = (
        jax.ShapeDtypeStruct((ROWS, D), BF),
        jax.ShapeDtypeStruct((ROWS, D), BF),
        jax.ShapeDtypeStruct((HALF, QC), F32),
        jax.ShapeDtypeStruct((HALF, HEAD), F32),
        jax.ShapeDtypeStruct((HALF, HEAD), F32),
        jax.ShapeDtypeStruct((HALF, QC), F32),
    )
    made = pl.pallas_call(
        kernel,
        out_shape=results,
        in_specs=[vmem, vmem, hbm, hbm, hbm, hbm, vmem],
        out_specs=(vmem,) * 6,
        scratch_shapes=[
            pltpu.VMEM((SEQ, D), BF),
            pltpu.VMEM((SEQ, D), BF),
            pltpu.VMEM((SEQ, SIDE), BF),
            pltpu.VMEM((D, 512), BF),
            pltpu.VMEM((QC, D), BF),
            pltpu.VMEM((SEQ, 512), BF),
            pltpu.VMEM((SEQ, QC), BF),
            pltpu.VMEM((SEQ, QC), BF),
            pltpu.VMEM((SEQ, 512), BF),
            pltpu.VMEM((SEQ, 512), BF),
            pltpu.VMEM((SEQ, 512), F32),
            pltpu.VMEM((2, SEQ, SEQ), F32),
            pltpu.VMEM((2, SEQ, SEQ), F32),
            pltpu.VMEM((D, QC), BF),
            pltpu.VMEM((2, SIDE, QC), BF),
            pltpu.VMEM((7, 2, HALF, QC), BF),
            pltpu.VMEM((2, 7, 2, HALF // 2, QC), BF),
            pltpu.VMEM((HALF, QC), BF),
            pltpu.VMEM((2, 8, 2, ROWS, D), BF),
            pltpu.VMEM((2, 8, ROWS, D), BF),
            pltpu.VMEM((2, 7, ROWS, D), BF),
            dma((4,)),
            dma((3, 16)),
            dma((3, 16)),
            dma((7, 2)),
            dma((7, 2)),
            dma((2, 7, 2)),
            dma((2, 7, 2)),
            dma((5,)),
            dma((5,)),
            dma((2,)),
            dma((2,)),
            dma((2, 8)),
            dma((2, 8)),
        ],
        compiler_params=pltpu.CompilerParams(
            collective_id=0, has_side_effects=True, vmem_limit_bytes=64 * 2**20 - 2**17
        ),
        cost_estimate=pl.CostEstimate(
            flops=12 * 10**9, bytes_accessed=10**7, transcendentals=10**6
        ),
    )(tokens, norm_gain, w_query, w_key, w_value, w_output, d_mixed)
    mixed, d_tokens, dw_query, dw_key, dw_value, dw_out_t = pl.pallas_call(
        hand_out,
        out_shape=results,
        in_specs=[pl.BlockSpec(memory_space=pltpu.HBM)] * 6,
        out_specs=(pl.BlockSpec(memory_space=pltpu.HBM),) * 6,
        scratch_shapes=[pltpu.VMEM(r.shape, r.dtype) for r in results] + [dma((2, 6))],
    )(*made)
    return (mixed, d_tokens, dw_query, dw_key, dw_value, dw_out_t.T)


def solution(mesh):
    return jax.shard_map(
        on_device,
        mesh=mesh,
        in_specs=(
            P(("dp", "tensor"), None),
            P(),
            P(None, "tensor"),
            P(None, "tensor"),
            P(None, "tensor"),
            P("tensor", None),
            P(("dp", "tensor"), None),
        ),
        out_specs=(
            P(("dp", "tensor"), None),
            P(("dp", "tensor"), None),
            P("dp", "tensor"),
            P("dp", "tensor"),
            P("dp", "tensor"),
            P("tensor", "dp"),
        ),
        check_vma=False,
    )
```

```python
import functools
import math

import jax
import jax.numpy as jnp
from jax import lax
from jax.experimental import pallas as pl
from jax.experimental.pallas import tpu as pltpu
from jax.sharding import PartitionSpec as P

D = 4608
HEADS = 32
HEAD = 128
SEQ = 512
ROWS = 32
QC = 256
CAP = 50.0
SCALE = 1.0 / math.sqrt(D // HEADS)
SIDE = D // 2
HALF = D // 16
THIRD = D // 3
QUARTER = D // 4
MESH = pl.DeviceIdType.MESH
BF = jnp.bfloat16
F32 = jnp.float32

AB = (((1,), (0,)), ((), ()))
ABT = (((1,), (1,)), ((), ()))
ATB = (((0,), (0,)), ((), ()))


def dot(a, b, dims=AB):
    return lax.dot_general(a, b, dims, preferred_element_type=F32)


def at(i, n):
    return pl.ds(pl.multiple_of(i * n, n), n)


def kernel(
    tok_h, gain_h, wq, wk, wv, wo, dm_h,
    mixed_o, dtok_o, dwq_o, dwk_o, dwv_o, dwo_o,
    tok, gain, dm, mixed, dtok, dwq, dwk, dwv, dwo, mix_sum,
    fn, fd, fx, w, wout, qkv, ctx, ctx_t, dctx, dqkv, dqkv_x, acc, probs, slope,
    grad_o, grad_i, recv_o, recv_i, recv_y, part, sib_in, far_in,
    in_sem, out_sem, ag_s, ag_r, hi_s, hi_r, zo_s, zo_r, zi_s, zi_r, y_s, y_r, sib_s, sib_r, far_s, far_r,
):
    dp, tensor = lax.axis_index("dp"), lax.axis_index("tensor")
    z, yh = lax.div(dp, 2), lax.rem(dp, 2)
    yl, x, c = lax.div(tensor, 8), lax.rem(lax.div(tensor, 2), 4), lax.rem(tensor, 2)

    def device(z_, yh_, yl_, x_, c_):
        return (z_ * 2 + yh_, yl_ * 8 + x_ * 2 + c_)

    def ring(i, step, n):
        return lax.rem(i + step + n, n)

    right = device(z, yh, yl, ring(x, 1, 4), c)
    left = device(z, yh, yl, ring(x, -1, 4), c)
    across = device(z, yh, 1 - yl, x, c)
    sibling = device(z, yh, yl, x, 1 - c)
    up = device(ring(z, 1, 8), yh, yl, x, c)
    down = device(ring(z, -1, 8), yh, yl, x, c)
    other_y = device(z, 1 - yh, yl, x, c)
    next_y = device(z, 1 - yh, 1 - yl, x, c)

    lead = lax.div(ring(z, 3, 8), 2)

    def quarter(j):
        return at(lax.rem(lead + j, 4), QUARTER)

    barrier = pltpu.get_barrier_semaphore()
    peers = (sibling, left, right, across, up, down, other_y, next_y)
    for peer in peers:
        pl.semaphore_signal(barrier, inc=1, device_id=peer, device_id_type=MESH)
    tok_in = pltpu.make_async_copy(tok_h, tok, in_sem.at[0])
    gain_in = pltpu.make_async_copy(gain_h, gain, in_sem.at[1])
    dm_in = pltpu.make_async_copy(dm_h, dm, in_sem.at[2])
    for copy in (tok_in, gain_in, dm_in):
        copy.start()

    def remote(src, dst, send_sem, recv_sem, to):
        return pltpu.make_async_remote_copy(
            src_ref=src, dst_ref=dst, send_sem=send_sem, recv_sem=recv_sem,
            device_id=to, device_id_type=MESH,
        )

    tok_in.wait()
    gain_in.wait()
    values = tok[...].astype(F32)
    scale = lax.rsqrt(jnp.mean(values * values, axis=-1, keepdims=True) + 1e-06)
    normed = values * scale * gain[...]
    mine = at(tensor, ROWS)
    sides = [
        jnp.concatenate(
            [normed[:, (2 * k + h) * HALF : (2 * k + h + 1) * HALF] for k in range(8)], axis=1
        )
        for h in range(2)
    ]
    fn[mine, :SIDE] = jnp.where(yh == 0, sides[1], sides[0]).astype(BF)
    fn[mine, SIDE:] = jnp.where(yh == 0, sides[0], sides[1]).astype(BF)
    dm_in.wait()
    for j in range(4):
        fd[mine, j * QUARTER : (j + 1) * QUARTER] = dm[:, quarter(j)]
    pl.semaphore_wait(barrier, len(peers))

    def block(dx, dy, core):
        return (yl if dy == 0 else 1 - yl) * 8 + ring(x, dx, 4) * 2 + core

    class Gather:
        order = ((0, 0), (-1, 0), (1, 0), (0, 1), (2, 0), (-1, 1), (1, 1), (2, 1))

        def __init__(self, full, a, first_column, columns):
            self.full, self.a = full, a
            self.columns = pl.ds(first_column, columns)

        def copy(self, i, rows, to):
            ref = self.full.at[rows, self.columns]
            return remote(ref, ref, ag_s.at[self.a, i], ag_r.at[self.a, i], to)

        def whole(self, dx, dy, core=c):
            return at(block(dx, dy, core), ROWS)

        def piece(self, dx, half):
            return at(block(dx, 0, c) * 2 + half, ROWS // 2)

        def to_sibling(self, i):
            self.copy(8 + i, self.whole(*self.order[i]), sibling).start()

        def step1(self):
            self.copy(0, self.whole(0, 0), right).start()
            self.copy(1, self.whole(0, 0), left).start()
            self.copy(2, self.whole(0, 0), across).start()
            self.to_sibling(0)

        def step2(self):
            self.copy(0, self.whole(-1, 0), right).wait_recv()
            self.copy(3, self.piece(-1, 0), right).start()
            self.copy(1, self.whole(1, 0), left).wait_recv()
            self.copy(4, self.piece(1, 1), left).start()
            self.copy(2, self.whole(0, 1), across).wait_recv()
            self.copy(5, self.whole(0, 1), right).start()
            self.copy(6, self.whole(0, 1), left).start()
            for i in (1, 2, 3):
                self.to_sibling(i)

        def step3(self):
            self.copy(3, self.piece(2, 0), right).wait_recv()
            self.copy(4, self.piece(2, 1), left).wait_recv()
            self.copy(7, self.whole(2, 0), across).start()
            self.to_sibling(4)

        def step4(self):
            self.copy(5, self.whole(-1, 1), right).wait_recv()
            self.to_sibling(5)
            self.copy(6, self.whole(1, 1), left).wait_recv()
            self.to_sibling(6)
            self.copy(7, self.whole(2, 1), across).wait_recv()
            self.to_sibling(7)

        def end(self):
            for i in range(8):
                self.copy(8 + i, self.whole(*self.order[i], 1 - c), sibling).wait_recv()

        def sent(self):
            for i, to in ((0, right), (1, left), (2, across), (5, right), (6, left), (7, across)):
                self.copy(i, self.whole(0, 0), to).wait_send()
            self.copy(3, self.piece(0, 0), right).wait_send()
            self.copy(4, self.piece(0, 0), left).wait_send()
            for i in range(8):
                self.copy(8 + i, self.whole(0, 0), sibling).wait_send()

    n = [Gather(fn, t, t * THIRD, THIRD) for t in range(3)]
    d_parts = ((0, 2 * QUARTER), (2 * QUARTER, QUARTER), (3 * QUARTER, QUARTER))
    d = [Gather(fd, 3 + t, *d_parts[t]) for t in range(3)]

    pieces = ((0, THIRD), (THIRD, SIDE - THIRD))

    def from_next(i):
        ref = (at(c, SEQ // 2), pl.ds(*pieces[i]))
        return remote(fn.at[ref], fx.at[ref], hi_s.at[i], hi_r.at[i], next_y)

    def from_sibling(i):
        ref = fx.at[at(c, SEQ // 2), pl.ds(*pieces[i])]
        return remote(ref, ref, hi_s.at[2 + i], hi_r.at[2 + i], sibling)

    def third(t):
        return slice(t * THIRD, (t + 1) * THIRD)

    def project(t):
        term = dot(fn[:, third(t)], w[third(t), :])
        if t == 0:
            acc[...] = term
        elif t == 1:
            acc[...] += term
        else:
            qkv[...] = (acc[...] + term).astype(BF)

    n[0].step1()
    n[1].step1()

    columns = (pl.ds(0, 256), pl.ds(256, 128), pl.ds(384, 128))
    for i, weight in enumerate((wq, wk, wv)):
        for h in range(2):
            for k in range(8):
                pltpu.make_async_copy(
                    weight.at[at(2 * k + lax.rem(yh + 1 + h, 2), HALF), :],
                    w.at[pl.ds((8 * h + k) * HALF, HALF), columns[i]],
                    in_sem.at[3 + i],
                ).start()
    for j in range(4):
        pltpu.make_async_copy(
            wo.at[:, quarter(j)], wout.at[:, pl.ds(j * QUARTER, QUARTER)], in_sem.at[6]
        ).start()

    n[0].step2()
    n[2].step1()
    n[0].step3()
    n[1].step2()
    d[0].step1()
    n[0].step4()
    n[1].step3()
    n[2].step2()
    n[0].end()
    for i, weight in enumerate((wq, wk, wv)):
        pltpu.make_async_copy(weight, w.at[:, columns[i]], in_sem.at[3 + i]).wait()
    project(0)
    from_next(0).start()
    n[1].step4()
    d[1].step1()
    n[2].step3()
    n[1].end()
    from_next(1).start()
    project(1)
    d[0].step2()
    n[2].step4()
    d[2].step1()
    n[2].end()
    project(2)

    blocks = ((0, 256), (256, 512))

    def attend(h):
        for lo, hi in blocks:
            q = qkv[lo:hi, h * HEAD : (h + 1) * HEAD]
            scores = dot(q, qkv[:hi, 256:384], ABT)
            th = jnp.tanh(scores * (SCALE / CAP))
            row = lax.broadcasted_iota(jnp.int32, (256, hi), 0) + lo
            col = lax.broadcasted_iota(jnp.int32, (256, hi), 1)
            weight = jnp.where(row >= col, jnp.exp(CAP * th), 0.0)
            p = weight * (1.0 / jnp.sum(weight, axis=-1, keepdims=True))
            probs[h, lo:hi, :hi] = p
            slope[h, lo:hi, :hi] = p * ((1.0 - th * th) * SCALE)
            ctx[lo:hi, h * HEAD : (h + 1) * HEAD] = dot(
                p.astype(BF), qkv[:hi, 384:512]
            ).astype(BF)

    attend(0)
    d[0].step3()
    d[1].step2()
    attend(1)
    ctx_t[...] = ctx[...].T

    class Scatter:
        moves = (
            (2, 1, 0, None, across),
            (1, 1, 1, None, right),
            (-1, 1, 2, None, left),
            (2, 0, 3, 0, right),
            (2, 0, 3, 1, left),
            (1, 0, 4, None, right),
            (-1, 0, 5, None, left),
            (0, 1, 6, None, across),
        )

        def __init__(self, a, t):
            self.a, self.t = a, t
            self.part, self.far = part.at[a, t], far_in.at[a, t]

        def chip(self, dx, dy):
            return (yl if dy == 0 else 1 - yl) * 4 + ring(x, dx, 4)

        def sib_copy(self):
            a, t = self.a, self.t
            return remote(
                part.at[a, t, :, 1 - c], sib_in.at[a, t], sib_s.at[a, t], sib_r.at[a, t], sibling
            )

        def copy(self, i):
            dx, dy, slot, half, to = self.moves[i]
            src, dst = self.part.at[self.chip(dx, dy), c], self.far.at[slot]
            if half is not None:
                rows = pl.ds(half * (ROWS // 2), ROWS // 2)
                src, dst = src.at[rows], dst.at[rows]
            return remote(src, dst, far_s.at[self.a, self.t, i], far_r.at[self.a, self.t, i], to)

        def add(self, dx, dy, slots, rows=slice(0, ROWS)):
            a, t, k = self.a, self.t, self.chip(dx, dy)
            total = part[a, t, k, c, rows].astype(F32)
            for slot in slots:
                total = total + far_in[a, t, slot, rows].astype(F32)
            part[a, t, k, c, rows] = total.astype(BF)

        def start(self, term):
            part[self.a, self.t] = term.astype(BF).reshape(8, 2, ROWS, THIRD)
            self.sib_copy().start()

        def spread(self):
            a, t = self.a, self.t
            self.sib_copy().wait()

            def one(k, carry):
                part[a, t, k, c] = part[a, t, k, c] + sib_in[a, t, k]
                return carry

            lax.fori_loop(0, 8, one, 0)
            for i in range(3):
                self.copy(i).start()

        def middle(self):
            self.copy(0).wait_recv()
            self.add(2, 0, (0,))
            self.copy(3).start()
            self.copy(4).start()
            self.copy(1).wait_recv()
            self.copy(2).wait_recv()
            self.add(0, 1, (1, 2))
            self.copy(7).start()

        def late(self):
            self.copy(3).wait_recv()
            self.add(1, 0, (3,), slice(0, ROWS // 2))
            self.copy(5).start()
            self.copy(4).wait_recv()
            self.add(-1, 0, (3,), slice(ROWS // 2, ROWS))
            self.copy(6).start()

        def total(self):
            a, t = self.a, self.t
            out = part[a, t, self.chip(0, 0), c].astype(F32)
            for i, slot in ((5, 4), (6, 5), (7, 6)):
                self.copy(i).wait_recv()
                out = out + far_in[a, t, slot].astype(F32)
            return out

        def sent(self):
            for i in range(8):
                self.copy(i).wait_send()

    m = [Scatter(0, t) for t in range(3)]
    g = [Scatter(1, t) for t in range(3)]

    away = (4, 3, 3, 2, 2, 1, 1)

    def chunk_o(k):
        return lax.rem(lax.div(k, 2) + 4 - lead, 4) * 2 + lax.rem(k, 2)

    def chunk_i(k):
        return k

    class Chain:
        def __init__(self, grad, recv, send_sem, recv_sem, half, chunk):
            self.grad, self.recv, self.send_sem, self.recv_sem = grad, recv, send_sem, recv_sem
            self.half, self.chunk = half, chunk

        def place(self, i, way, distance):
            part_of = way if i % 2 == 0 else 1 - way
            k = self.chunk(ring(z, distance * (1 - 2 * way), 8))
            return at(k * 2 + part_of, self.half)

        def copy(self, i, way):
            return remote(
                self.grad.at[self.place(i, way, away[i]), :], self.recv.at[i, way],
                self.send_sem.at[i, way], self.recv_sem.at[i, way], (up, down)[way],
            )

        def arrive(self, i, way):
            self.copy(i, way).wait_recv()
            here = self.place(i, way, away[i] - 1)
            self.grad[here, :] = self.grad[here, :] + self.recv[i, way]

        def start(self):
            for i in range(2):
                for way in range(2):
                    self.copy(i, way).start()

        def step(self, i):
            for way in range(2):
                self.arrive(i - 2, way)
                self.copy(i, way).start()

        def end(self):
            for i in (5, 6):
                for way in range(2):
                    self.arrive(i, way)

        def sent(self):
            for i in range(7):
                for way in range(2):
                    self.copy(i, way).wait_send()

    zo = Chain(grad_o, recv_o, zo_s, zo_r, HALF, chunk_o)
    zq = Chain(grad_i.at[0], recv_i.at[0], zi_s.at[0], zi_r.at[0], HALF // 2, chunk_i)
    zk = Chain(grad_i.at[1], recv_i.at[1], zi_s.at[1], zi_r.at[1], HALF // 2, chunk_i)

    def grad_out(t):
        first, size = d_parts[t]
        cols = slice(first, first + size)
        grad_o[cols, :] = dot(ctx_t[...], fd[:, cols]).astype(BF).T

    def back_out(t):
        first, size = d_parts[t]
        cols = slice(first, first + size)
        term = dot(fd[:, cols], wout[:, cols], ABT)
        if t == 0:
            acc[:, :QC] = term
        elif t == 1:
            acc[:, :QC] += term
        else:
            dctx[...] = (acc[:, :QC] + term).astype(BF)

    pltpu.make_async_copy(wo, wout, in_sem.at[6]).wait()
    d[2].step2()
    d[0].step4()
    d[1].step3()
    for t in range(3):
        m[t].start(dot(ctx[...], wout[:, third(t)]))
    d[0].end()
    grad_out(0)
    zo.start()
    back_out(0)
    d[1].step4()
    d[2].step3()
    d[1].end()
    grad_out(1)
    back_out(1)
    from_next(0).wait_recv()
    from_sibling(0).start()
    zo.step(2)
    d[2].step4()
    d[2].end()
    back_out(2)

    def pair_copy(i):
        cols = (pl.ds(0, 128), pl.ds(128, 128), pl.ds(256, 256))[i]
        return remote(
            dqkv.at[:, cols], dqkv_x.at[:, cols], y_s.at[2 + i], y_r.at[2 + i], other_y
        )

    acc[...] = jnp.zeros_like(acc)

    def attend_back(h):
        for lo, hi in blocks:
            heads = slice(h * HEAD, (h + 1) * HEAD)
            d_ctx = dctx[lo:hi, heads]
            p = probs[h, lo:hi, :hi]
            d_p = dot(d_ctx, qkv[:hi, 384:512], ABT)
            inner = jnp.sum(p * d_p, axis=-1, keepdims=True)
            d_s = (slope[h, lo:hi, :hi] * (d_p - inner)).astype(BF)
            dqkv[lo:hi, heads] = dot(d_s, qkv[:hi, 256:384]).astype(BF)
            acc[:hi, 256:384] += dot(d_s, qkv[lo:hi, heads], ATB)
            acc[:hi, 384:512] += dot(p.astype(BF), d_ctx, ATB)
        pair_copy(h).start()

    attend_back(0)
    attend_back(1)
    dqkv[:, 256:512] = acc[:, 256:512].astype(BF)
    pair_copy(2).start()
    for t in range(3):
        m[t].spread()
    grad_out(2)
    zo.step(3)
    from_next(1).wait_recv()
    from_sibling(1).start()

    def back_in(t):
        g[t].start(dot(dqkv[...], w[third(t), :], ABT))

    back_in(0)
    back_in(1)
    m[0].middle()
    zo.step(4)
    back_in(2)
    m[1].middle()
    m[2].middle()
    g[0].spread()
    g[1].spread()
    zo.step(5)
    m[0].late()
    m[1].late()
    g[2].spread()
    zo.step(6)
    m[2].late()
    for i in range(2):
        from_sibling(i).wait_recv()
    for i in range(3):
        pair_copy(i).wait_recv()

    own_t = dqkv[...].T
    pair_t = dqkv_x[...].T
    for i in range(2):
        rows = slice(i * QUARTER, (i + 1) * QUARTER)
        own = slice(SIDE + i * QUARTER, SIDE + (i + 1) * QUARTER)
        term = (dot(own_t, fn[:, own]) + dot(pair_t, fx[:, rows])).astype(BF)
        grad_i[0, rows, :] = term[:256].T
        grad_i[1, rows, :] = term[256:].T
    zq.start()
    zk.start()

    def keep(h):
        return at(chunk_o(z) * 2 + h, HALF)

    g[0].middle()
    zo.end()
    y_copy = remote(grad_o.at[keep(1 - yh), :], recv_y, y_s.at[0], y_r.at[0], other_y)
    y_copy.start()
    zq.step(2)
    zk.step(2)
    g[1].middle()
    for t in range(3):
        mix_sum[:, third(t)] = m[t].total()
    for j in range(4):
        mixed[:, quarter(j)] = (
            tok[:, quarter(j)].astype(F32) + mix_sum[:, j * QUARTER : (j + 1) * QUARTER]
        ).astype(BF)
    mixed_out = pltpu.make_async_copy(mixed, mixed_o, out_sem.at[0])
    mixed_out.start()
    g[0].late()
    zq.step(3)
    zk.step(3)
    g[2].middle()
    g[1].late()
    zq.step(4)
    zk.step(4)
    for gather in n + d:
        gather.sent()
    g[2].late()
    zq.step(5)
    zk.step(5)
    y_copy.wait()
    dwo[...] = grad_o[keep(yh), :].astype(F32) + recv_y[...].astype(F32)
    dwo_out = pltpu.make_async_copy(dwo, dwo_o, out_sem.at[5])
    dwo_out.start()
    for stream in m:
        stream.sent()
    zo.sent()
    zq.step(6)
    zk.step(6)

    sums = [g[t].total() for t in range(3)]
    summed = jnp.concatenate(sums, axis=1)
    first = jnp.where(yh == 0, summed[:, SIDE:], summed[:, :SIDE])
    second = jnp.where(yh == 0, summed[:, :SIDE], summed[:, SIDE:])
    d_normed = jnp.concatenate(
        [
            side[:, k * HALF : (k + 1) * HALF]
            for k in range(8)
            for side in (first, second)
        ],
        axis=1,
    )
    upstream = gain[...] * d_normed
    values = tok[...].astype(F32)
    scale = lax.rsqrt(jnp.mean(values * values, axis=-1, keepdims=True) + 1e-06)
    back_norm = scale * upstream - values * (scale * scale * scale) * jnp.mean(
        upstream * values, axis=-1, keepdims=True
    )
    dtok[...] = (dm[...].astype(F32) + back_norm).astype(BF)
    dtok_out = pltpu.make_async_copy(dtok, dtok_o, out_sem.at[1])
    dtok_out.start()

    zq.end()
    dwq[...] = grad_i[0, at(z, HALF), :].astype(F32)
    dwq_out = pltpu.make_async_copy(dwq, dwq_o, out_sem.at[2])
    dwq_out.start()
    zk.end()
    dwk[...] = grad_i[1, at(z, HALF), :HEAD].astype(F32)
    dwv[...] = grad_i[1, at(z, HALF), HEAD:].astype(F32)
    dwk_out = pltpu.make_async_copy(dwk, dwk_o, out_sem.at[3])
    dwk_out.start()
    dwv_out = pltpu.make_async_copy(dwv, dwv_o, out_sem.at[4])
    dwv_out.start()

    for stream in g:
        stream.sent()
    zq.sent()
    zk.sent()
    for i in range(2):
        from_next(i).wait_send()
        from_sibling(i).wait_send()
    for i in range(3):
        pair_copy(i).wait_send()
    for copy in (mixed_out, dtok_out, dwq_out, dwk_out, dwv_out, dwo_out):
        copy.wait()


def hand_out(*refs):
    sources, results, held, sem = refs[:6], refs[6:12], refs[12:18], refs[18]
    loads = [
        pltpu.make_async_copy(source, ref, sem.at[0, i])
        for i, (source, ref) in enumerate(zip(sources, held))
    ]
    stores = [
        pltpu.make_async_copy(ref, result, sem.at[1, i])
        for i, (ref, result) in enumerate(zip(held, results))
    ]
    for load in loads:
        load.start()
    for load, store in zip(loads, stores):
        load.wait()
        store.start()
    for store in stores:
        store.wait()


def on_device(tokens, norm_gain, w_query, w_key, w_value, w_output, d_mixed):
    hbm = pl.BlockSpec(memory_space=pltpu.HBM)
    dma = pltpu.SemaphoreType.DMA
    results = (
        jax.ShapeDtypeStruct((ROWS, D), BF),
        jax.ShapeDtypeStruct((ROWS, D), BF),
        jax.ShapeDtypeStruct((HALF, QC), F32),
        jax.ShapeDtypeStruct((HALF, HEAD), F32),
        jax.ShapeDtypeStruct((HALF, HEAD), F32),
        jax.ShapeDtypeStruct((HALF, QC), F32),
    )
    made = pl.pallas_call(
        kernel,
        out_shape=results,
        in_specs=[hbm] * 7,
        out_specs=(hbm,) * 6,
        scratch_shapes=[
            pltpu.VMEM((ROWS, D), BF),
            pltpu.VMEM((D,), F32),
            pltpu.VMEM((ROWS, D), BF),
            *(pltpu.VMEM(r.shape, r.dtype) for r in results),
            pltpu.VMEM((ROWS, D), F32),
            pltpu.VMEM((SEQ, D), BF),
            pltpu.VMEM((SEQ, D), BF),
            pltpu.VMEM((SEQ, SIDE), BF),
            pltpu.VMEM((D, 512), BF),
            pltpu.VMEM((QC, D), BF),
            pltpu.VMEM((SEQ, 512), BF),
            pltpu.VMEM((SEQ, QC), BF),
            pltpu.VMEM((QC, SEQ), BF),
            pltpu.VMEM((SEQ, QC), BF),
            pltpu.VMEM((SEQ, 512), BF),
            pltpu.VMEM((SEQ, 512), BF),
            pltpu.VMEM((SEQ, 512), F32),
            pltpu.VMEM((2, SEQ, SEQ), F32),
            pltpu.VMEM((2, SEQ, SEQ), F32),
            pltpu.VMEM((D, QC), BF),
            pltpu.VMEM((2, SIDE, QC), BF),
            pltpu.VMEM((7, 2, HALF, QC), BF),
            pltpu.VMEM((2, 7, 2, HALF // 2, QC), BF),
            pltpu.VMEM((HALF, QC), BF),
            pltpu.VMEM((2, 3, 8, 2, ROWS, THIRD), BF),
            pltpu.VMEM((2, 3, 8, ROWS, THIRD), BF),
            pltpu.VMEM((2, 3, 7, ROWS, THIRD), BF),
            dma((7,)),
            dma((6,)),
            dma((6, 16)),
            dma((6, 16)),
            dma((4,)),
            dma((4,)),
            dma((7, 2)),
            dma((7, 2)),
            dma((2, 7, 2)),
            dma((2, 7, 2)),
            dma((5,)),
            dma((5,)),
            dma((2, 3)),
            dma((2, 3)),
            dma((2, 3, 8)),
            dma((2, 3, 8)),
        ],
        compiler_params=pltpu.CompilerParams(
            collective_id=0, has_side_effects=True, vmem_limit_bytes=64 * 2**20 - 2**17
        ),
        cost_estimate=pl.CostEstimate(
            flops=12 * 10**9, bytes_accessed=10**7, transcendentals=10**6
        ),
    )(tokens, norm_gain, w_query, w_key, w_value, w_output, d_mixed)
    mixed, d_tokens, dw_query, dw_key, dw_value, dw_out_t = pl.pallas_call(
        hand_out,
        out_shape=results,
        in_specs=[hbm] * 6,
        out_specs=(hbm,) * 6,
        scratch_shapes=[pltpu.VMEM(r.shape, r.dtype) for r in results] + [dma((2, 6))],
    )(*made)
    return (mixed, d_tokens, dw_query, dw_key, dw_value, dw_out_t.T)


def solution(mesh):
    return jax.shard_map(
        on_device,
        mesh=mesh,
        in_specs=(
            P(("dp", "tensor"), None),
            P(),
            P(None, "tensor"),
            P(None, "tensor"),
            P(None, "tensor"),
            P("tensor", None),
            P(("dp", "tensor"), None),
        ),
        out_specs=(
            P(("dp", "tensor"), None),
            P(("dp", "tensor"), None),
            P("dp", "tensor"),
            P("dp", "tensor"),
            P("dp", "tensor"),
            P("tensor", "dp"),
        ),
        check_vma=False,
    )
```

```python
import functools
import math

import jax
import jax.numpy as jnp
from jax import lax
from jax.experimental import pallas as pl
from jax.experimental.pallas import tpu as pltpu
from jax.sharding import PartitionSpec as P

D = 4608
HEADS = 32
HEAD = 128
SEQ = 512
ROWS = 32
QC = 256
CAP = 50.0
SCALE = 1.0 / math.sqrt(D // HEADS)
SIDE = D // 2
HALF = D // 16
THIRD = D // 3
QUARTER = D // 4
MESH = pl.DeviceIdType.MESH
BF = jnp.bfloat16
F32 = jnp.float32

AB = (((1,), (0,)), ((), ()))
ABT = (((1,), (1,)), ((), ()))
ATB = (((0,), (0,)), ((), ()))


def dot(a, b, dims=AB):
    return lax.dot_general(a, b, dims, preferred_element_type=F32)


def at(i, n):
    return pl.ds(pl.multiple_of(i * n, n), n)


def kernel(
    tok_h, gain_h, wq, wk, wv, wo, dm_h,
    mixed_o, dtok_o, dwq_o, dwk_o, dwv_o, dwo_o,
    tok, gain, dm, mixed, dtok, dwq, dwk, dwv, dwo, mix_sum,
    fn, fd, fx, w, wout, qkv, ctx, ctx_t, dctx, dqkv, dqkv_x, acc, probs, slope,
    grad_o, grad_i, recv_o, recv_i, recv_y, part, sib_in, far_in,
    in_sem, out_sem, ag_s, ag_r, hi_s, hi_r, zo_s, zo_r, zi_s, zi_r, y_s, y_r, sib_s, sib_r, far_s, far_r,
):
    dp, tensor = lax.axis_index("dp"), lax.axis_index("tensor")
    z, yh = lax.div(dp, 2), lax.rem(dp, 2)
    yl, x, c = lax.div(tensor, 8), lax.rem(lax.div(tensor, 2), 4), lax.rem(tensor, 2)

    def device(z_, yh_, yl_, x_, c_):
        return (z_ * 2 + yh_, yl_ * 8 + x_ * 2 + c_)

    def ring(i, step, n):
        return lax.rem(i + step + n, n)

    right = device(z, yh, yl, ring(x, 1, 4), c)
    left = device(z, yh, yl, ring(x, -1, 4), c)
    across = device(z, yh, 1 - yl, x, c)
    sibling = device(z, yh, yl, x, 1 - c)
    up = device(ring(z, 1, 8), yh, yl, x, c)
    down = device(ring(z, -1, 8), yh, yl, x, c)
    other_y = device(z, 1 - yh, yl, x, c)
    next_y = device(z, 1 - yh, 1 - yl, x, c)

    lead = lax.div(ring(z, 3, 8), 2)

    def quarter(j):
        return at(lax.rem(lead + j, 4), QUARTER)

    barrier = pltpu.get_barrier_semaphore()
    peers = (sibling, left, right, across, up, down, other_y, next_y)
    for peer in peers:
        pl.semaphore_signal(barrier, inc=1, device_id=peer, device_id_type=MESH)
    tok_in = pltpu.make_async_copy(tok_h, tok, in_sem.at[0])
    gain_in = pltpu.make_async_copy(gain_h, gain, in_sem.at[1])
    dm_in = pltpu.make_async_copy(dm_h, dm, in_sem.at[2])
    for copy in (tok_in, gain_in, dm_in):
        copy.start()

    def remote(src, dst, send_sem, recv_sem, to):
        return pltpu.make_async_remote_copy(
            src_ref=src, dst_ref=dst, send_sem=send_sem, recv_sem=recv_sem,
            device_id=to, device_id_type=MESH,
        )

    tok_in.wait()
    gain_in.wait()
    values = tok[...].astype(F32)
    scale = lax.rsqrt(jnp.mean(values * values, axis=-1, keepdims=True) + 1e-06)
    normed = values * scale * gain[...]
    mine = at(tensor, ROWS)
    sides = [
        jnp.concatenate(
            [normed[:, (2 * k + h) * HALF : (2 * k + h + 1) * HALF] for k in range(8)], axis=1
        )
        for h in range(2)
    ]
    fn[mine, :SIDE] = jnp.where(yh == 0, sides[1], sides[0]).astype(BF)
    fn[mine, SIDE:] = jnp.where(yh == 0, sides[0], sides[1]).astype(BF)
    dm_in.wait()
    for j in range(4):
        fd[mine, j * QUARTER : (j + 1) * QUARTER] = dm[:, quarter(j)]
    pl.semaphore_wait(barrier, len(peers))

    def block(dx, dy, core):
        return (yl if dy == 0 else 1 - yl) * 8 + ring(x, dx, 4) * 2 + core

    class Gather:
        order = ((0, 0), (-1, 0), (1, 0), (0, 1), (2, 0), (-1, 1), (1, 1), (2, 1))

        def __init__(self, full, a, first_column, columns):
            self.full, self.a = full, a
            self.columns = pl.ds(first_column, columns)

        def copy(self, i, rows, to):
            ref = self.full.at[rows, self.columns]
            return remote(ref, ref, ag_s.at[self.a, i], ag_r.at[self.a, i], to)

        def whole(self, dx, dy, core=c):
            return at(block(dx, dy, core), ROWS)

        def piece(self, dx, half):
            return at(block(dx, 0, c) * 2 + half, ROWS // 2)

        def to_sibling(self, i):
            self.copy(8 + i, self.whole(*self.order[i]), sibling).start()

        def step1(self):
            self.copy(0, self.whole(0, 0), right).start()
            self.copy(1, self.whole(0, 0), left).start()
            self.copy(2, self.whole(0, 0), across).start()
            self.to_sibling(0)

        def step2(self):
            self.copy(0, self.whole(-1, 0), right).wait_recv()
            self.copy(3, self.piece(-1, 0), right).start()
            self.copy(1, self.whole(1, 0), left).wait_recv()
            self.copy(4, self.piece(1, 1), left).start()
            self.copy(2, self.whole(0, 1), across).wait_recv()
            self.copy(5, self.whole(0, 1), right).start()
            self.copy(6, self.whole(0, 1), left).start()
            for i in (1, 2, 3):
                self.to_sibling(i)

        def step3(self):
            self.copy(3, self.piece(2, 0), right).wait_recv()
            self.copy(4, self.piece(2, 1), left).wait_recv()
            self.copy(7, self.whole(2, 0), across).start()
            self.to_sibling(4)

        def step4(self):
            self.copy(5, self.whole(-1, 1), right).wait_recv()
            self.to_sibling(5)
            self.copy(6, self.whole(1, 1), left).wait_recv()
            self.to_sibling(6)
            self.copy(7, self.whole(2, 1), across).wait_recv()
            self.to_sibling(7)

        def end(self):
            for i in range(8):
                self.copy(8 + i, self.whole(*self.order[i], 1 - c), sibling).wait_recv()

        def sent(self):
            for i, to in ((0, right), (1, left), (2, across), (5, right), (6, left), (7, across)):
                self.copy(i, self.whole(0, 0), to).wait_send()
            self.copy(3, self.piece(0, 0), right).wait_send()
            self.copy(4, self.piece(0, 0), left).wait_send()
            for i in range(8):
                self.copy(8 + i, self.whole(0, 0), sibling).wait_send()

    n = [Gather(fn, t, t * THIRD, THIRD) for t in range(3)]
    d_parts = ((0, 2 * QUARTER), (2 * QUARTER, QUARTER), (3 * QUARTER, QUARTER))
    d = [Gather(fd, 3 + t, *d_parts[t]) for t in range(3)]

    pieces = ((0, THIRD), (THIRD, SIDE - THIRD))

    def from_next(i):
        ref = (at(c, SEQ // 2), pl.ds(*pieces[i]))
        return remote(fn.at[ref], fx.at[ref], hi_s.at[i], hi_r.at[i], next_y)

    def from_sibling(i):
        ref = fx.at[at(c, SEQ // 2), pl.ds(*pieces[i])]
        return remote(ref, ref, hi_s.at[2 + i], hi_r.at[2 + i], sibling)

    def third(t):
        return slice(t * THIRD, (t + 1) * THIRD)

    def project(t):
        term = dot(fn[:, third(t)], w[third(t), :])
        if t == 0:
            acc[...] = term
        elif t == 1:
            acc[...] += term
        else:
            qkv[...] = (acc[...] + term).astype(BF)

    n[0].step1()
    n[1].step1()

    columns = (pl.ds(0, 256), pl.ds(256, 128), pl.ds(384, 128))
    for i, weight in enumerate((wq, wk, wv)):
        for h in range(2):
            for k in range(8):
                pltpu.make_async_copy(
                    weight.at[at(2 * k + lax.rem(yh + 1 + h, 2), HALF), :],
                    w.at[pl.ds((8 * h + k) * HALF, HALF), columns[i]],
                    in_sem.at[3 + i],
                ).start()
    for j in range(4):
        pltpu.make_async_copy(
            wo.at[:, quarter(j)], wout.at[:, pl.ds(j * QUARTER, QUARTER)], in_sem.at[6]
        ).start()

    n[0].step2()
    n[2].step1()
    n[0].step3()
    n[1].step2()
    d[0].step1()
    n[0].step4()
    n[1].step3()
    n[2].step2()
    n[0].end()
    for i, weight in enumerate((wq, wk, wv)):
        pltpu.make_async_copy(weight, w.at[:, columns[i]], in_sem.at[3 + i]).wait()
    project(0)
    from_next(0).start()
    n[1].step4()
    d[1].step1()
    n[2].step3()
    n[1].end()
    from_next(1).start()
    project(1)
    d[0].step2()
    n[2].step4()
    d[2].step1()
    n[2].end()
    project(2)

    blocks = ((0, 256), (256, 512))

    def attend(h):
        for lo, hi in blocks:
            q = qkv[lo:hi, h * HEAD : (h + 1) * HEAD]
            scores = dot(q, qkv[:hi, 256:384], ABT)
            th = jnp.tanh(scores * (SCALE / CAP))
            row = lax.broadcasted_iota(jnp.int32, (256, hi), 0) + lo
            col = lax.broadcasted_iota(jnp.int32, (256, hi), 1)
            weight = jnp.where(row >= col, jnp.exp(CAP * th), 0.0)
            p = weight * (1.0 / jnp.sum(weight, axis=-1, keepdims=True))
            probs[h, lo:hi, :hi] = p
            slope[h, lo:hi, :hi] = p * ((1.0 - th * th) * SCALE)
            ctx[lo:hi, h * HEAD : (h + 1) * HEAD] = dot(
                p.astype(BF), qkv[:hi, 384:512]
            ).astype(BF)

    attend(0)
    d[0].step3()
    d[1].step2()
    attend(1)
    ctx_t[...] = ctx[...].T

    class Scatter:
        moves = (
            (2, 1, 0, None, across),
            (1, 1, 1, None, right),
            (-1, 1, 2, None, left),
            (2, 0, 3, 0, right),
            (2, 0, 3, 1, left),
            (1, 0, 4, None, right),
            (-1, 0, 5, None, left),
            (0, 1, 6, None, across),
        )

        def __init__(self, a, t):
            self.a, self.t = a, t
            self.part, self.far = part.at[a, t], far_in.at[a, t]

        def chip(self, dx, dy):
            return (yl if dy == 0 else 1 - yl) * 4 + ring(x, dx, 4)

        def sib_copy(self):
            a, t = self.a, self.t
            return remote(
                part.at[a, t, :, 1 - c], sib_in.at[a, t], sib_s.at[a, t], sib_r.at[a, t], sibling
            )

        def copy(self, i):
            dx, dy, slot, half, to = self.moves[i]
            src, dst = self.part.at[self.chip(dx, dy), c], self.far.at[slot]
            if half is not None:
                rows = pl.ds(half * (ROWS // 2), ROWS // 2)
                src, dst = src.at[rows], dst.at[rows]
            return remote(src, dst, far_s.at[self.a, self.t, i], far_r.at[self.a, self.t, i], to)

        def add(self, dx, dy, slots, rows=slice(0, ROWS)):
            a, t, k = self.a, self.t, self.chip(dx, dy)
            total = part[a, t, k, c, rows].astype(F32)
            for slot in slots:
                total = total + far_in[a, t, slot, rows].astype(F32)
            part[a, t, k, c, rows] = total.astype(BF)

        def start(self, term):
            part[self.a, self.t] = term.astype(BF).reshape(8, 2, ROWS, THIRD)
            self.sib_copy().start()

        def spread(self):
            a, t = self.a, self.t
            self.sib_copy().wait()

            def one(k, carry):
                part[a, t, k, c] = part[a, t, k, c] + sib_in[a, t, k]
                return carry

            lax.fori_loop(0, 8, one, 0)
            for i in range(3):
                self.copy(i).start()

        def middle(self):
            self.copy(0).wait_recv()
            self.add(2, 0, (0,))
            self.copy(3).start()
            self.copy(4).start()
            self.copy(1).wait_recv()
            self.copy(2).wait_recv()
            self.add(0, 1, (1, 2))
            self.copy(7).start()

        def late(self):
            self.copy(3).wait_recv()
            self.add(1, 0, (3,), slice(0, ROWS // 2))
            self.copy(5).start()
            self.copy(4).wait_recv()
            self.add(-1, 0, (3,), slice(ROWS // 2, ROWS))
            self.copy(6).start()

        def total(self):
            a, t = self.a, self.t
            out = part[a, t, self.chip(0, 0), c].astype(F32)
            for i, slot in ((5, 4), (6, 5), (7, 6)):
                self.copy(i).wait_recv()
                out = out + far_in[a, t, slot].astype(F32)
            return out

        def sent(self):
            for i in range(8):
                self.copy(i).wait_send()

    m = [Scatter(0, t) for t in range(3)]
    g = [Scatter(1, t) for t in range(3)]

    away = (4, 3, 3, 2, 2, 1, 1)

    def chunk_o(k):
        return lax.rem(lax.div(k, 2) + 4 - lead, 4) * 2 + lax.rem(k, 2)

    def chunk_i(k):
        return k

    class Chain:
        def __init__(self, grad, recv, send_sem, recv_sem, half, chunk):
            self.grad, self.recv, self.send_sem, self.recv_sem = grad, recv, send_sem, recv_sem
            self.half, self.chunk = half, chunk

        def place(self, i, way, distance):
            part_of = way if i % 2 == 0 else 1 - way
            k = self.chunk(ring(z, distance * (1 - 2 * way), 8))
            return at(k * 2 + part_of, self.half)

        def copy(self, i, way):
            return remote(
                self.grad.at[self.place(i, way, away[i]), :], self.recv.at[i, way],
                self.send_sem.at[i, way], self.recv_sem.at[i, way], (up, down)[way],
            )

        def arrive(self, i, way):
            self.copy(i, way).wait_recv()
            here = self.place(i, way, away[i] - 1)
            self.grad[here, :] = self.grad[here, :] + self.recv[i, way]

        def start(self):
            for i in range(2):
                for way in range(2):
                    self.copy(i, way).start()

        def step(self, i):
            for way in range(2):
                self.arrive(i - 2, way)
                self.copy(i, way).start()

        def end(self):
            for i in (5, 6):
                for way in range(2):
                    self.arrive(i, way)

        def sent(self):
            for i in range(7):
                for way in range(2):
                    self.copy(i, way).wait_send()

    zo = Chain(grad_o, recv_o, zo_s, zo_r, HALF, chunk_o)
    zq = Chain(grad_i.at[0], recv_i.at[0], zi_s.at[0], zi_r.at[0], HALF // 2, chunk_i)
    zk = Chain(grad_i.at[1], recv_i.at[1], zi_s.at[1], zi_r.at[1], HALF // 2, chunk_i)

    def grad_out(t):
        first, size = d_parts[t]
        cols = slice(first, first + size)
        grad_o[cols, :] = dot(ctx_t[...], fd[:, cols]).astype(BF).T

    def back_out(t):
        first, size = d_parts[t]
        cols = slice(first, first + size)
        term = dot(fd[:, cols], wout[:, cols], ABT)
        if t == 0:
            acc[:, :QC] = term
        elif t == 1:
            acc[:, :QC] += term
        else:
            dctx[...] = (acc[:, :QC] + term).astype(BF)

    pltpu.make_async_copy(wo, wout, in_sem.at[6]).wait()
    d[2].step2()
    d[0].step4()
    d[1].step3()
    for t in range(3):
        m[t].start(dot(ctx[...], wout[:, third(t)]))
    d[0].end()
    grad_out(0)
    zo.start()
    back_out(0)
    d[1].step4()
    d[2].step3()
    m[0].spread()
    d[1].end()
    grad_out(1)
    back_out(1)
    m[1].spread()
    zo.step(2)
    d[2].step4()
    m[2].spread()
    d[2].end()
    grad_out(2)
    zo.step(3)
    back_out(2)

    def pair_copy(i):
        cols = (pl.ds(0, 128), pl.ds(128, 128), pl.ds(256, 256))[i]
        return remote(
            dqkv.at[:, cols], dqkv_x.at[:, cols], y_s.at[2 + i], y_r.at[2 + i], other_y
        )

    acc[...] = jnp.zeros_like(acc)

    def attend_back(h):
        for lo, hi in blocks:
            heads = slice(h * HEAD, (h + 1) * HEAD)
            d_ctx = dctx[lo:hi, heads]
            p = probs[h, lo:hi, :hi]
            d_p = dot(d_ctx, qkv[:hi, 384:512], ABT)
            inner = jnp.sum(p * d_p, axis=-1, keepdims=True)
            d_s = (slope[h, lo:hi, :hi] * (d_p - inner)).astype(BF)
            dqkv[lo:hi, heads] = dot(d_s, qkv[:hi, 256:384]).astype(BF)
            acc[:hi, 256:384] += dot(d_s, qkv[lo:hi, heads], ATB)
            acc[:hi, 384:512] += dot(p.astype(BF), d_ctx, ATB)
        pair_copy(h).start()

    attend_back(0)
    zo.step(4)
    attend_back(1)
    dqkv[:, 256:512] = acc[:, 256:512].astype(BF)
    pair_copy(2).start()
    from_next(0).wait_recv()
    from_sibling(0).start()

    def back_in(t):
        g[t].start(dot(dqkv[...], w[third(t), :], ABT))

    back_in(0)
    zo.step(5)
    back_in(1)
    m[0].middle()
    back_in(2)
    zo.step(6)
    from_next(1).wait_recv()
    from_sibling(1).start()
    m[1].middle()
    m[2].middle()
    g[0].spread()
    m[0].late()
    g[1].spread()
    for i in range(2):
        from_sibling(i).wait_recv()

    def grad_in(which):
        cols = slice(which * QC, (which + 1) * QC)
        own_t = dqkv[:, cols].T
        pair_t = dqkv_x[:, cols].T
        for i in range(2):
            rows = slice(i * QUARTER, (i + 1) * QUARTER)
            own = slice(SIDE + i * QUARTER, SIDE + (i + 1) * QUARTER)
            term = dot(own_t, fn[:, own]) + dot(pair_t, fx[:, rows])
            grad_i[which, rows, :] = term.astype(BF).T

    pair_copy(0).wait_recv()
    pair_copy(1).wait_recv()
    grad_in(0)
    zq.start()
    g[2].spread()
    m[1].late()
    m[2].late()
    zq.step(2)
    zq.step(3)
    pair_copy(2).wait_recv()
    grad_in(1)
    zk.start()

    def keep(h):
        return at(chunk_o(z) * 2 + h, HALF)

    g[0].middle()
    zo.end()
    y_copy = remote(grad_o.at[keep(1 - yh), :], recv_y, y_s.at[0], y_r.at[0], other_y)
    y_copy.start()
    g[1].middle()
    zq.step(4)
    zk.step(2)
    g[2].middle()
    zq.step(5)
    for t in range(3):
        mix_sum[:, third(t)] = m[t].total()
    for j in range(4):
        mixed[:, quarter(j)] = (
            tok[:, quarter(j)].astype(F32) + mix_sum[:, j * QUARTER : (j + 1) * QUARTER]
        ).astype(BF)
    mixed_out = pltpu.make_async_copy(mixed, mixed_o, out_sem.at[0])
    mixed_out.start()
    zk.step(3)
    g[0].late()
    zq.step(6)
    zk.step(4)
    g[1].late()
    g[2].late()
    zk.step(5)
    y_copy.wait()
    dwo[...] = grad_o[keep(yh), :].astype(F32) + recv_y[...].astype(F32)
    dwo_out = pltpu.make_async_copy(dwo, dwo_o, out_sem.at[5])
    dwo_out.start()
    for gather in n + d:
        gather.sent()
    for stream in m:
        stream.sent()
    zo.sent()
    zk.step(6)
    zq.end()
    dwq[...] = grad_i[0, at(z, HALF), :].astype(F32)
    dwq_out = pltpu.make_async_copy(dwq, dwq_o, out_sem.at[2])
    dwq_out.start()

    sums = [g[t].total() for t in range(3)]
    summed = jnp.concatenate(sums, axis=1)
    first = jnp.where(yh == 0, summed[:, SIDE:], summed[:, :SIDE])
    second = jnp.where(yh == 0, summed[:, :SIDE], summed[:, SIDE:])
    d_normed = jnp.concatenate(
        [
            side[:, k * HALF : (k + 1) * HALF]
            for k in range(8)
            for side in (first, second)
        ],
        axis=1,
    )
    upstream = gain[...] * d_normed
    values = tok[...].astype(F32)
    scale = lax.rsqrt(jnp.mean(values * values, axis=-1, keepdims=True) + 1e-06)
    back_norm = scale * upstream - values * (scale * scale * scale) * jnp.mean(
        upstream * values, axis=-1, keepdims=True
    )
    dtok[...] = (dm[...].astype(F32) + back_norm).astype(BF)
    dtok_out = pltpu.make_async_copy(dtok, dtok_o, out_sem.at[1])
    dtok_out.start()

    zk.end()
    dwk[...] = grad_i[1, at(z, HALF), :HEAD].astype(F32)
    dwv[...] = grad_i[1, at(z, HALF), HEAD:].astype(F32)
    dwk_out = pltpu.make_async_copy(dwk, dwk_o, out_sem.at[3])
    dwk_out.start()
    dwv_out = pltpu.make_async_copy(dwv, dwv_o, out_sem.at[4])
    dwv_out.start()

    for stream in g:
        stream.sent()
    zq.sent()
    zk.sent()
    for i in range(2):
        from_next(i).wait_send()
        from_sibling(i).wait_send()
    for i in range(3):
        pair_copy(i).wait_send()
    for copy in (mixed_out, dtok_out, dwq_out, dwk_out, dwv_out, dwo_out):
        copy.wait()


def hand_out(*refs):
    sources, results, held, sem = refs[:6], refs[6:12], refs[12:18], refs[18]
    loads = [
        pltpu.make_async_copy(source, ref, sem.at[0, i])
        for i, (source, ref) in enumerate(zip(sources, held))
    ]
    stores = [
        pltpu.make_async_copy(ref, result, sem.at[1, i])
        for i, (ref, result) in enumerate(zip(held, results))
    ]
    for load in loads:
        load.start()
    for load, store in zip(loads, stores):
        load.wait()
        store.start()
    for store in stores:
        store.wait()


def on_device(tokens, norm_gain, w_query, w_key, w_value, w_output, d_mixed):
    hbm = pl.BlockSpec(memory_space=pltpu.HBM)
    dma = pltpu.SemaphoreType.DMA
    results = (
        jax.ShapeDtypeStruct((ROWS, D), BF),
        jax.ShapeDtypeStruct((ROWS, D), BF),
        jax.ShapeDtypeStruct((HALF, QC), F32),
        jax.ShapeDtypeStruct((HALF, HEAD), F32),
        jax.ShapeDtypeStruct((HALF, HEAD), F32),
        jax.ShapeDtypeStruct((HALF, QC), F32),
    )
    made = pl.pallas_call(
        kernel,
        out_shape=results,
        in_specs=[hbm] * 7,
        out_specs=(hbm,) * 6,
        scratch_shapes=[
            pltpu.VMEM((ROWS, D), BF),
            pltpu.VMEM((D,), F32),
            pltpu.VMEM((ROWS, D), BF),
            *(pltpu.VMEM(r.shape, r.dtype) for r in results),
            pltpu.VMEM((ROWS, D), F32),
            pltpu.VMEM((SEQ, D), BF),
            pltpu.VMEM((SEQ, D), BF),
            pltpu.VMEM((SEQ, SIDE), BF),
            pltpu.VMEM((D, 512), BF),
            pltpu.VMEM((QC, D), BF),
            pltpu.VMEM((SEQ, 512), BF),
            pltpu.VMEM((SEQ, QC), BF),
            pltpu.VMEM((QC, SEQ), BF),
            pltpu.VMEM((SEQ, QC), BF),
            pltpu.VMEM((SEQ, 512), BF),
            pltpu.VMEM((SEQ, 512), BF),
            pltpu.VMEM((SEQ, 512), F32),
            pltpu.VMEM((2, SEQ, SEQ), F32),
            pltpu.VMEM((2, SEQ, SEQ), F32),
            pltpu.VMEM((D, QC), BF),
            pltpu.VMEM((2, SIDE, QC), BF),
            pltpu.VMEM((7, 2, HALF, QC), BF),
            pltpu.VMEM((2, 7, 2, HALF // 2, QC), BF),
            pltpu.VMEM((HALF, QC), BF),
            pltpu.VMEM((2, 3, 8, 2, ROWS, THIRD), BF),
            pltpu.VMEM((2, 3, 8, ROWS, THIRD), BF),
            pltpu.VMEM((2, 3, 7, ROWS, THIRD), BF),
            dma((7,)),
            dma((6,)),
            dma((6, 16)),
            dma((6, 16)),
            dma((4,)),
            dma((4,)),
            dma((7, 2)),
            dma((7, 2)),
            dma((2, 7, 2)),
            dma((2, 7, 2)),
            dma((5,)),
            dma((5,)),
            dma((2, 3)),
            dma((2, 3)),
            dma((2, 3, 8)),
            dma((2, 3, 8)),
        ],
        compiler_params=pltpu.CompilerParams(
            collective_id=0, has_side_effects=True, vmem_limit_bytes=64 * 2**20 - 2**17
        ),
        cost_estimate=pl.CostEstimate(
            flops=12 * 10**9, bytes_accessed=10**7, transcendentals=10**6
        ),
    )(tokens, norm_gain, w_query, w_key, w_value, w_output, d_mixed)
    mixed, d_tokens, dw_query, dw_key, dw_value, dw_out_t = pl.pallas_call(
        hand_out,
        out_shape=results,
        in_specs=[hbm] * 6,
        out_specs=(hbm,) * 6,
        scratch_shapes=[pltpu.VMEM(r.shape, r.dtype) for r in results] + [dma((2, 6))],
    )(*made)
    return (mixed, d_tokens, dw_query, dw_key, dw_value, dw_out_t.T)


def solution(mesh):
    return jax.shard_map(
        on_device,
        mesh=mesh,
        in_specs=(
            P(("dp", "tensor"), None),
            P(),
            P(None, "tensor"),
            P(None, "tensor"),
            P(None, "tensor"),
            P("tensor", None),
            P(("dp", "tensor"), None),
        ),
        out_specs=(
            P(("dp", "tensor"), None),
            P(("dp", "tensor"), None),
            P("dp", "tensor"),
            P("dp", "tensor"),
            P("dp", "tensor"),
            P("tensor", "dp"),
        ),
        check_vma=False,
    )
```

```python
import functools
import math

import jax
import jax.numpy as jnp
from jax import lax
from jax.experimental import pallas as pl
from jax.experimental.pallas import tpu as pltpu
from jax.sharding import PartitionSpec as P

D = 4608
HEADS = 32
HEAD = 128
SEQ = 512
ROWS = 32
QC = 256
CAP = 50.0
SCALE = 1.0 / math.sqrt(D // HEADS)
SIDE = D // 2
HALF = D // 16
THIRD = D // 3
QUARTER = D // 4
MESH = pl.DeviceIdType.MESH
BF = jnp.bfloat16
F32 = jnp.float32

AB = (((1,), (0,)), ((), ()))
ABT = (((1,), (1,)), ((), ()))
ATB = (((0,), (0,)), ((), ()))


def dot(a, b, dims=AB):
    return lax.dot_general(a, b, dims, preferred_element_type=F32)


def at(i, n):
    return pl.ds(pl.multiple_of(i * n, n), n)


def kernel(
    tok_h, gain_h, wq, wk, wv, wo, dm_h,
    mixed_o, dtok_o, dwq_o, dwk_o, dwv_o, dwo_o,
    tok, gain, dm, mixed, dtok, dwq, dwk, dwv, dwo, mix_sum,
    fn, fd, fx, w, wout, qkv, ctx, ctx_t, dctx, dqkv, dqkv_x, acc, probs, slope,
    grad_o, grad_i, recv_o, recv_i, recv_y, part, sib_in, far_in,
    in_sem, out_sem, ag_s, ag_r, hi_s, hi_r, zo_s, zo_r, zi_s, zi_r, y_s, y_r, sib_s, sib_r, far_s, far_r,
):
    dp, tensor = lax.axis_index("dp"), lax.axis_index("tensor")
    z, yh = lax.div(dp, 2), lax.rem(dp, 2)
    yl, x, c = lax.div(tensor, 8), lax.rem(lax.div(tensor, 2), 4), lax.rem(tensor, 2)

    def device(z_, yh_, yl_, x_, c_):
        return (z_ * 2 + yh_, yl_ * 8 + x_ * 2 + c_)

    def ring(i, step, n):
        return lax.rem(i + step + n, n)

    right = device(z, yh, yl, ring(x, 1, 4), c)
    left = device(z, yh, yl, ring(x, -1, 4), c)
    across = device(z, yh, 1 - yl, x, c)
    sibling = device(z, yh, yl, x, 1 - c)
    up = device(ring(z, 1, 8), yh, yl, x, c)
    down = device(ring(z, -1, 8), yh, yl, x, c)
    other_y = device(z, 1 - yh, yl, x, c)
    next_y = device(z, 1 - yh, 1 - yl, x, c)

    lead = lax.div(ring(z, 3, 8), 2)

    def quarter(j):
        return at(lax.rem(lead + j, 4), QUARTER)

    barrier = pltpu.get_barrier_semaphore()
    peers = (sibling, left, right, across, up, down, other_y, next_y)
    for peer in peers:
        pl.semaphore_signal(barrier, inc=1, device_id=peer, device_id_type=MESH)
    tok_in = pltpu.make_async_copy(tok_h, tok, in_sem.at[0])
    gain_in = pltpu.make_async_copy(gain_h, gain, in_sem.at[1])
    dm_in = pltpu.make_async_copy(dm_h, dm, in_sem.at[2])
    for copy in (tok_in, gain_in, dm_in):
        copy.start()

    def remote(src, dst, send_sem, recv_sem, to):
        return pltpu.make_async_remote_copy(
            src_ref=src, dst_ref=dst, send_sem=send_sem, recv_sem=recv_sem,
            device_id=to, device_id_type=MESH,
        )

    tok_in.wait()
    gain_in.wait()
    values = tok[...].astype(F32)
    scale = lax.rsqrt(jnp.mean(values * values, axis=-1, keepdims=True) + 1e-06)
    normed = values * scale * gain[...]
    mine = at(tensor, ROWS)
    sides = [
        jnp.concatenate(
            [normed[:, (2 * k + h) * HALF : (2 * k + h + 1) * HALF] for k in range(8)], axis=1
        )
        for h in range(2)
    ]
    fn[mine, :SIDE] = jnp.where(yh == 0, sides[1], sides[0]).astype(BF)
    fn[mine, SIDE:] = jnp.where(yh == 0, sides[0], sides[1]).astype(BF)
    dm_in.wait()
    for j in range(4):
        fd[mine, j * QUARTER : (j + 1) * QUARTER] = dm[:, quarter(j)]

    columns = (pl.ds(0, 256), pl.ds(256, 128), pl.ds(384, 128))
    for i, weight in enumerate((wq, wk, wv)):
        for h in range(2):
            for k in range(8):
                pltpu.make_async_copy(
                    weight.at[at(2 * k + lax.rem(yh + 1 + h, 2), HALF), :],
                    w.at[pl.ds((8 * h + k) * HALF, HALF), columns[i]],
                    in_sem.at[3 + i],
                ).start()
    for j in range(4):
        pltpu.make_async_copy(
            wo.at[:, quarter(j)], wout.at[:, pl.ds(j * QUARTER, QUARTER)], in_sem.at[6]
        ).start()
    pl.semaphore_wait(barrier, len(peers))

    def block(dx, dy, core):
        return (yl if dy == 0 else 1 - yl) * 8 + ring(x, dx, 4) * 2 + core

    class Gather:
        order = ((0, 0), (-1, 0), (1, 0), (0, 1), (2, 0), (-1, 1), (1, 1), (2, 1))

        def __init__(self, full, a, first_column, columns):
            self.full, self.a = full, a
            self.columns = pl.ds(first_column, columns)

        def copy(self, i, rows, to):
            ref = self.full.at[rows, self.columns]
            return remote(ref, ref, ag_s.at[self.a, i], ag_r.at[self.a, i], to)

        def whole(self, dx, dy, core=c):
            return at(block(dx, dy, core), ROWS)

        def piece(self, dx, half):
            return at(block(dx, 0, c) * 2 + half, ROWS // 2)

        def to_sibling(self, i):
            self.copy(8 + i, self.whole(*self.order[i]), sibling).start()

        def step1(self):
            self.copy(0, self.whole(0, 0), right).start()
            self.copy(1, self.whole(0, 0), left).start()
            self.copy(2, self.whole(0, 0), across).start()
            self.to_sibling(0)

        def step2(self):
            self.copy(0, self.whole(-1, 0), right).wait_recv()
            self.copy(3, self.piece(-1, 0), right).start()
            self.copy(1, self.whole(1, 0), left).wait_recv()
            self.copy(4, self.piece(1, 1), left).start()
            self.copy(2, self.whole(0, 1), across).wait_recv()
            self.copy(5, self.whole(0, 1), right).start()
            self.copy(6, self.whole(0, 1), left).start()
            for i in (1, 2, 3):
                self.to_sibling(i)

        def step3(self):
            self.copy(3, self.piece(2, 0), right).wait_recv()
            self.copy(4, self.piece(2, 1), left).wait_recv()
            self.copy(7, self.whole(2, 0), across).start()
            self.to_sibling(4)

        def step4(self):
            self.copy(5, self.whole(-1, 1), right).wait_recv()
            self.to_sibling(5)
            self.copy(6, self.whole(1, 1), left).wait_recv()
            self.to_sibling(6)
            self.copy(7, self.whole(2, 1), across).wait_recv()
            self.to_sibling(7)

        def end(self):
            for i in range(8):
                self.copy(8 + i, self.whole(*self.order[i], 1 - c), sibling).wait_recv()

        def sent(self):
            for i, to in ((0, right), (1, left), (2, across), (5, right), (6, left), (7, across)):
                self.copy(i, self.whole(0, 0), to).wait_send()
            self.copy(3, self.piece(0, 0), right).wait_send()
            self.copy(4, self.piece(0, 0), left).wait_send()
            for i in range(8):
                self.copy(8 + i, self.whole(0, 0), sibling).wait_send()

    n = [Gather(fn, t, t * THIRD, THIRD) for t in range(3)]
    d_parts = ((0, 2 * QUARTER), (2 * QUARTER, QUARTER), (3 * QUARTER, QUARTER))
    d = [Gather(fd, 3 + t, *d_parts[t]) for t in range(3)]

    pieces = ((0, THIRD), (THIRD, SIDE - THIRD))

    def from_next(i):
        ref = (at(c, SEQ // 2), pl.ds(*pieces[i]))
        return remote(fn.at[ref], fx.at[ref], hi_s.at[i], hi_r.at[i], next_y)

    def from_sibling(i):
        ref = fx.at[at(c, SEQ // 2), pl.ds(*pieces[i])]
        return remote(ref, ref, hi_s.at[2 + i], hi_r.at[2 + i], sibling)

    def third(t):
        return slice(t * THIRD, (t + 1) * THIRD)

    def project(t):
        term = dot(fn[:, third(t)], w[third(t), :])
        if t == 0:
            acc[...] = term
        elif t == 1:
            acc[...] += term
        else:
            qkv[...] = (acc[...] + term).astype(BF)

    n[0].step1()
    n[1].step1()

    n[0].step2()
    n[2].step1()
    n[0].step3()
    n[1].step2()
    d[0].step1()
    n[0].step4()
    n[1].step3()
    n[2].step2()
    n[0].end()
    for i, weight in enumerate((wq, wk, wv)):
        pltpu.make_async_copy(weight, w.at[:, columns[i]], in_sem.at[3 + i]).wait()
    project(0)
    from_next(0).start()
    n[1].step4()
    d[1].step1()
    n[2].step3()
    n[1].end()
    from_next(1).start()
    project(1)
    d[0].step2()
    n[2].step4()
    d[2].step1()
    n[2].end()
    project(2)

    blocks = ((0, 256), (256, 512))

    def attend(h):
        for lo, hi in blocks:
            q = qkv[lo:hi, h * HEAD : (h + 1) * HEAD]
            scores = dot(q, qkv[:hi, 256:384], ABT)
            th = jnp.tanh(scores * (SCALE / CAP))
            row = lax.broadcasted_iota(jnp.int32, (256, hi), 0) + lo
            col = lax.broadcasted_iota(jnp.int32, (256, hi), 1)
            weight = jnp.where(row >= col, jnp.exp(CAP * th), 0.0)
            p = weight * (1.0 / jnp.sum(weight, axis=-1, keepdims=True))
            probs[h, lo:hi, :hi] = p
            slope[h, lo:hi, :hi] = p * ((1.0 - th * th) * SCALE)
            ctx[lo:hi, h * HEAD : (h + 1) * HEAD] = dot(
                p.astype(BF), qkv[:hi, 384:512]
            ).astype(BF)

    attend(0)
    d[0].step3()
    d[1].step2()
    attend(1)
    ctx_t[...] = ctx[...].T

    class Scatter:
        moves = (
            (2, 1, 0, None, across),
            (1, 1, 1, None, right),
            (-1, 1, 2, None, left),
            (2, 0, 3, 0, right),
            (2, 0, 3, 1, left),
            (1, 0, 4, None, right),
            (-1, 0, 5, None, left),
            (0, 1, 6, None, across),
        )

        def __init__(self, a, t):
            self.a, self.t = a, t
            self.part, self.far = part.at[a, t], far_in.at[a, t]

        def chip(self, dx, dy):
            return (yl if dy == 0 else 1 - yl) * 4 + ring(x, dx, 4)

        def sib_copy(self):
            a, t = self.a, self.t
            return remote(
                part.at[a, t, :, 1 - c], sib_in.at[a, t], sib_s.at[a, t], sib_r.at[a, t], sibling
            )

        def copy(self, i):
            dx, dy, slot, half, to = self.moves[i]
            src, dst = self.part.at[self.chip(dx, dy), c], self.far.at[slot]
            if half is not None:
                rows = pl.ds(half * (ROWS // 2), ROWS // 2)
                src, dst = src.at[rows], dst.at[rows]
            return remote(src, dst, far_s.at[self.a, self.t, i], far_r.at[self.a, self.t, i], to)

        def add(self, dx, dy, slots, rows=slice(0, ROWS)):
            a, t, k = self.a, self.t, self.chip(dx, dy)
            total = part[a, t, k, c, rows].astype(F32)
            for slot in slots:
                total = total + far_in[a, t, slot, rows].astype(F32)
            part[a, t, k, c, rows] = total.astype(BF)

        def start(self, term):
            part[self.a, self.t] = term.astype(BF).reshape(8, 2, ROWS, THIRD)
            self.sib_copy().start()

        def spread(self):
            a, t = self.a, self.t
            self.sib_copy().wait()

            def one(k, carry):
                part[a, t, k, c] = part[a, t, k, c] + sib_in[a, t, k]
                return carry

            lax.fori_loop(0, 8, one, 0)
            for i in range(3):
                self.copy(i).start()

        def middle(self):
            self.copy(0).wait_recv()
            self.add(2, 0, (0,))
            self.copy(3).start()
            self.copy(4).start()
            self.copy(1).wait_recv()
            self.copy(2).wait_recv()
            self.add(0, 1, (1, 2))
            self.copy(7).start()

        def late(self):
            self.copy(3).wait_recv()
            self.add(1, 0, (3,), slice(0, ROWS // 2))
            self.copy(5).start()
            self.copy(4).wait_recv()
            self.add(-1, 0, (3,), slice(ROWS // 2, ROWS))
            self.copy(6).start()

        def total(self):
            a, t = self.a, self.t
            out = part[a, t, self.chip(0, 0), c].astype(F32)
            for i, slot in ((5, 4), (6, 5), (7, 6)):
                self.copy(i).wait_recv()
                out = out + far_in[a, t, slot].astype(F32)
            return out

        def sent(self):
            for i in range(8):
                self.copy(i).wait_send()

    m = [Scatter(0, t) for t in range(3)]
    g = [Scatter(1, t) for t in range(3)]

    away = (4, 3, 3, 2, 2, 1, 1)

    def chunk_o(k):
        return lax.rem(lax.div(k, 2) + 4 - lead, 4) * 2 + lax.rem(k, 2)

    def chunk_i(k):
        return k

    class Chain:
        def __init__(self, grad, recv, send_sem, recv_sem, half, chunk):
            self.grad, self.recv, self.send_sem, self.recv_sem = grad, recv, send_sem, recv_sem
            self.half, self.chunk = half, chunk

        def place(self, i, way, distance):
            part_of = way if i % 2 == 0 else 1 - way
            k = self.chunk(ring(z, distance * (1 - 2 * way), 8))
            return at(k * 2 + part_of, self.half)

        def copy(self, i, way):
            return remote(
                self.grad.at[self.place(i, way, away[i]), :], self.recv.at[i, way],
                self.send_sem.at[i, way], self.recv_sem.at[i, way], (up, down)[way],
            )

        def arrive(self, i, way):
            self.copy(i, way).wait_recv()
            here = self.place(i, way, away[i] - 1)
            self.grad[here, :] = self.grad[here, :] + self.recv[i, way]

        def start(self):
            for i in range(2):
                for way in range(2):
                    self.copy(i, way).start()

        def step(self, i):
            for way in range(2):
                self.arrive(i - 2, way)
                self.copy(i, way).start()

        def end(self):
            for i in (5, 6):
                for way in range(2):
                    self.arrive(i, way)

        def sent(self):
            for i in range(7):
                for way in range(2):
                    self.copy(i, way).wait_send()

    zo = Chain(grad_o, recv_o, zo_s, zo_r, HALF, chunk_o)
    zq = Chain(grad_i.at[0], recv_i.at[0], zi_s.at[0], zi_r.at[0], HALF // 2, chunk_i)
    zk = Chain(grad_i.at[1], recv_i.at[1], zi_s.at[1], zi_r.at[1], HALF // 2, chunk_i)

    def grad_out(t):
        first, size = d_parts[t]
        cols = slice(first, first + size)
        grad_o[cols, :] = dot(ctx_t[...], fd[:, cols]).astype(BF).T

    def back_out(t):
        first, size = d_parts[t]
        cols = slice(first, first + size)
        term = dot(fd[:, cols], wout[:, cols], ABT)
        if t == 0:
            acc[:, :QC] = term
        elif t == 1:
            acc[:, :QC] += term
        else:
            dctx[...] = (acc[:, :QC] + term).astype(BF)

    pltpu.make_async_copy(wo, wout, in_sem.at[6]).wait()
    d[2].step2()
    d[0].step4()
    d[1].step3()
    for t in range(3):
        m[t].start(dot(ctx[...], wout[:, third(t)]))
    d[0].end()
    grad_out(0)
    zo.start()
    back_out(0)
    d[1].step4()
    d[2].step3()
    m[0].spread()
    d[1].end()
    grad_out(1)
    back_out(1)
    m[1].spread()
    zo.step(2)
    d[2].step4()
    m[2].spread()
    d[2].end()
    grad_out(2)
    zo.step(3)
    back_out(2)

    def pair_copy(i):
        cols = (pl.ds(0, 128), pl.ds(128, 128), pl.ds(256, 256))[i]
        return remote(
            dqkv.at[:, cols], dqkv_x.at[:, cols], y_s.at[2 + i], y_r.at[2 + i], other_y
        )

    acc[...] = jnp.zeros_like(acc)

    def attend_back(h):
        for lo, hi in blocks:
            heads = slice(h * HEAD, (h + 1) * HEAD)
            d_ctx = dctx[lo:hi, heads]
            p = probs[h, lo:hi, :hi]
            d_p = dot(d_ctx, qkv[:hi, 384:512], ABT)
            inner = jnp.sum(p * d_p, axis=-1, keepdims=True)
            d_s = (slope[h, lo:hi, :hi] * (d_p - inner)).astype(BF)
            dqkv[lo:hi, heads] = dot(d_s, qkv[:hi, 256:384]).astype(BF)
            acc[:hi, 256:384] += dot(d_s, qkv[lo:hi, heads], ATB)
            acc[:hi, 384:512] += dot(p.astype(BF), d_ctx, ATB)
        pair_copy(h).start()

    attend_back(0)
    zo.step(4)
    attend_back(1)
    dqkv[:, 256:512] = acc[:, 256:512].astype(BF)
    pair_copy(2).start()
    from_next(0).wait_recv()
    from_sibling(0).start()

    def back_in(t):
        g[t].start(dot(dqkv[...], w[third(t), :], ABT))

    back_in(0)
    zo.step(5)
    back_in(1)
    m[0].middle()
    back_in(2)
    zo.step(6)
    from_next(1).wait_recv()
    from_sibling(1).start()
    m[1].middle()
    g[0].spread()
    m[2].middle()
    g[1].spread()
    g[2].spread()
    for i in range(2):
        from_sibling(i).wait_recv()

    def grad_in(which):
        cols = slice(which * QC, (which + 1) * QC)
        own_t = dqkv[:, cols].T
        pair_t = dqkv_x[:, cols].T
        for i in range(2):
            rows = slice(i * QUARTER, (i + 1) * QUARTER)
            own = slice(SIDE + i * QUARTER, SIDE + (i + 1) * QUARTER)
            term = dot(own_t, fn[:, own]) + dot(pair_t, fx[:, rows])
            grad_i[which, rows, :] = term.astype(BF).T

    pair_copy(0).wait_recv()
    pair_copy(1).wait_recv()
    grad_in(0)
    zq.start()
    m[0].late()
    m[1].late()
    zq.step(2)
    m[2].late()
    zq.step(3)
    pair_copy(2).wait_recv()
    grad_in(1)
    zk.start()
    zq.step(4)

    def keep(h):
        return at(chunk_o(z) * 2 + h, HALF)

    zo.end()
    zk.step(2)
    g[0].middle()
    zq.step(5)
    g[1].middle()
    zk.step(3)
    g[2].middle()
    zq.step(6)
    y_copy = remote(grad_o.at[keep(1 - yh), :], recv_y, y_s.at[0], y_r.at[0], other_y)
    y_copy.start()
    g[0].late()
    zk.step(4)
    for t in range(3):
        mix_sum[:, third(t)] = m[t].total()
    for j in range(4):
        mixed[:, quarter(j)] = (
            tok[:, quarter(j)].astype(F32) + mix_sum[:, j * QUARTER : (j + 1) * QUARTER]
        ).astype(BF)
    mixed_out = pltpu.make_async_copy(mixed, mixed_o, out_sem.at[0])
    mixed_out.start()
    g[1].late()
    zk.step(5)
    g[2].late()
    for gather in n + d:
        gather.sent()
    for stream in m:
        stream.sent()
    zo.sent()
    zk.step(6)
    y_copy.wait()
    dwo[...] = grad_o[keep(yh), :].astype(F32) + recv_y[...].astype(F32)
    dwo_out = pltpu.make_async_copy(dwo, dwo_o, out_sem.at[5])
    dwo_out.start()
    zq.end()
    dwq[...] = grad_i[0, at(z, HALF), :].astype(F32)
    dwq_out = pltpu.make_async_copy(dwq, dwq_o, out_sem.at[2])
    dwq_out.start()

    sums = [g[t].total() for t in range(3)]
    summed = jnp.concatenate(sums, axis=1)
    first = jnp.where(yh == 0, summed[:, SIDE:], summed[:, :SIDE])
    second = jnp.where(yh == 0, summed[:, :SIDE], summed[:, SIDE:])
    d_normed = jnp.concatenate(
        [
            side[:, k * HALF : (k + 1) * HALF]
            for k in range(8)
            for side in (first, second)
        ],
        axis=1,
    )
    upstream = gain[...] * d_normed
    values = tok[...].astype(F32)
    scale = lax.rsqrt(jnp.mean(values * values, axis=-1, keepdims=True) + 1e-06)
    back_norm = scale * upstream - values * (scale * scale * scale) * jnp.mean(
        upstream * values, axis=-1, keepdims=True
    )
    dtok[...] = (dm[...].astype(F32) + back_norm).astype(BF)
    dtok_out = pltpu.make_async_copy(dtok, dtok_o, out_sem.at[1])
    dtok_out.start()

    zk.end()
    dwk[...] = grad_i[1, at(z, HALF), :HEAD].astype(F32)
    dwv[...] = grad_i[1, at(z, HALF), HEAD:].astype(F32)
    dwk_out = pltpu.make_async_copy(dwk, dwk_o, out_sem.at[3])
    dwk_out.start()
    dwv_out = pltpu.make_async_copy(dwv, dwv_o, out_sem.at[4])
    dwv_out.start()

    for stream in g:
        stream.sent()
    zq.sent()
    zk.sent()
    for i in range(2):
        from_next(i).wait_send()
        from_sibling(i).wait_send()
    for i in range(3):
        pair_copy(i).wait_send()
    for copy in (mixed_out, dtok_out, dwq_out, dwk_out, dwv_out, dwo_out):
        copy.wait()


def hand_out(*refs):
    sources, results, held, sem = refs[:6], refs[6:12], refs[12:18], refs[18]
    loads = [
        pltpu.make_async_copy(source, ref, sem.at[0, i])
        for i, (source, ref) in enumerate(zip(sources, held))
    ]
    stores = [
        pltpu.make_async_copy(ref, result, sem.at[1, i])
        for i, (ref, result) in enumerate(zip(held, results))
    ]
    for load in loads:
        load.start()
    for load, store in zip(loads, stores):
        load.wait()
        store.start()
    for store in stores:
        store.wait()


def on_device(tokens, norm_gain, w_query, w_key, w_value, w_output, d_mixed):
    hbm = pl.BlockSpec(memory_space=pltpu.HBM)
    dma = pltpu.SemaphoreType.DMA
    results = (
        jax.ShapeDtypeStruct((ROWS, D), BF),
        jax.ShapeDtypeStruct((ROWS, D), BF),
        jax.ShapeDtypeStruct((HALF, QC), F32),
        jax.ShapeDtypeStruct((HALF, HEAD), F32),
        jax.ShapeDtypeStruct((HALF, HEAD), F32),
        jax.ShapeDtypeStruct((HALF, QC), F32),
    )
    made = pl.pallas_call(
        kernel,
        out_shape=results,
        in_specs=[hbm] * 7,
        out_specs=(hbm,) * 6,
        scratch_shapes=[
            pltpu.VMEM((ROWS, D), BF),
            pltpu.VMEM((D,), F32),
            pltpu.VMEM((ROWS, D), BF),
            *(pltpu.VMEM(r.shape, r.dtype) for r in results),
            pltpu.VMEM((ROWS, D), F32),
            pltpu.VMEM((SEQ, D), BF),
            pltpu.VMEM((SEQ, D), BF),
            pltpu.VMEM((SEQ, SIDE), BF),
            pltpu.VMEM((D, 512), BF),
            pltpu.VMEM((QC, D), BF),
            pltpu.VMEM((SEQ, 512), BF),
            pltpu.VMEM((SEQ, QC), BF),
            pltpu.VMEM((QC, SEQ), BF),
            pltpu.VMEM((SEQ, QC), BF),
            pltpu.VMEM((SEQ, 512), BF),
            pltpu.VMEM((SEQ, 512), BF),
            pltpu.VMEM((SEQ, 512), F32),
            pltpu.VMEM((2, SEQ, SEQ), F32),
            pltpu.VMEM((2, SEQ, SEQ), F32),
            pltpu.VMEM((D, QC), BF),
            pltpu.VMEM((2, SIDE, QC), BF),
            pltpu.VMEM((7, 2, HALF, QC), BF),
            pltpu.VMEM((2, 7, 2, HALF // 2, QC), BF),
            pltpu.VMEM((HALF, QC), BF),
            pltpu.VMEM((2, 3, 8, 2, ROWS, THIRD), BF),
            pltpu.VMEM((2, 3, 8, ROWS, THIRD), BF),
            pltpu.VMEM((2, 3, 7, ROWS, THIRD), BF),
            dma((7,)),
            dma((6,)),
            dma((6, 16)),
            dma((6, 16)),
            dma((4,)),
            dma((4,)),
            dma((7, 2)),
            dma((7, 2)),
            dma((2, 7, 2)),
            dma((2, 7, 2)),
            dma((5,)),
            dma((5,)),
            dma((2, 3)),
            dma((2, 3)),
            dma((2, 3, 8)),
            dma((2, 3, 8)),
        ],
        compiler_params=pltpu.CompilerParams(
            collective_id=0, has_side_effects=True, vmem_limit_bytes=64 * 2**20 - 2**17
        ),
        cost_estimate=pl.CostEstimate(
            flops=12 * 10**9, bytes_accessed=10**7, transcendentals=10**6
        ),
    )(tokens, norm_gain, w_query, w_key, w_value, w_output, d_mixed)
    mixed, d_tokens, dw_query, dw_key, dw_value, dw_out_t = pl.pallas_call(
        hand_out,
        out_shape=results,
        in_specs=[hbm] * 6,
        out_specs=(hbm,) * 6,
        scratch_shapes=[pltpu.VMEM(r.shape, r.dtype) for r in results] + [dma((2, 6))],
    )(*made)
    return (mixed, d_tokens, dw_query, dw_key, dw_value, dw_out_t.T)


def solution(mesh):
    return jax.shard_map(
        on_device,
        mesh=mesh,
        in_specs=(
            P(("dp", "tensor"), None),
            P(),
            P(None, "tensor"),
            P(None, "tensor"),
            P(None, "tensor"),
            P("tensor", None),
            P(("dp", "tensor"), None),
        ),
        out_specs=(
            P(("dp", "tensor"), None),
            P(("dp", "tensor"), None),
            P("dp", "tensor"),
            P("dp", "tensor"),
            P("dp", "tensor"),
            P("tensor", "dp"),
        ),
        check_vma=False,
    )
```

```python
import functools
import math

import jax
import jax.numpy as jnp
from jax import lax
from jax.experimental import pallas as pl
from jax.experimental.pallas import tpu as pltpu
from jax.sharding import PartitionSpec as P

D = 4608
HEADS = 32
HEAD = 128
SEQ = 512
ROWS = 32
QC = 256
CAP = 50.0
SCALE = 1.0 / math.sqrt(D // HEADS)
SIDE = D // 2
HALF = D // 16
THIRD = D // 3
QUARTER = D // 4
MESH = pl.DeviceIdType.MESH
BF = jnp.bfloat16
F32 = jnp.float32

AB = (((1,), (0,)), ((), ()))
ABT = (((1,), (1,)), ((), ()))
ATB = (((0,), (0,)), ((), ()))


def dot(a, b, dims=AB):
    return lax.dot_general(a, b, dims, preferred_element_type=F32)


def at(i, n):
    return pl.ds(pl.multiple_of(i * n, n), n)


def kernel(
    tok_h, gain_h, wq, wk, wv, wo, dm_h,
    mixed_o, dtok_o, dwq_o, dwk_o, dwv_o, dwo_o,
    tok, gain, dm, mixed, dtok, dwq, dwk, dwv, dwo, mix_sum,
    fn, fd, fx, w, wout, qkv, ctx, ctx_t, dctx, dqkv, dqkv_x, acc, probs, slope,
    grad_o, grad_i, recv_o, recv_i, recv_y, part, sib_in, far_in,
    in_sem, out_sem, ag_s, ag_r, hi_s, hi_r, zo_s, zo_r, zi_s, zi_r, y_s, y_r, sib_s, sib_r, far_s, far_r,
):
    dp, tensor = lax.axis_index("dp"), lax.axis_index("tensor")
    z, yh = lax.div(dp, 2), lax.rem(dp, 2)
    yl, x, c = lax.div(tensor, 8), lax.rem(lax.div(tensor, 2), 4), lax.rem(tensor, 2)

    def device(z_, yh_, yl_, x_, c_):
        return (z_ * 2 + yh_, yl_ * 8 + x_ * 2 + c_)

    def ring(i, step, n):
        return lax.rem(i + step + n, n)

    right = device(z, yh, yl, ring(x, 1, 4), c)
    left = device(z, yh, yl, ring(x, -1, 4), c)
    across = device(z, yh, 1 - yl, x, c)
    sibling = device(z, yh, yl, x, 1 - c)
    up = device(ring(z, 1, 8), yh, yl, x, c)
    down = device(ring(z, -1, 8), yh, yl, x, c)
    other_y = device(z, 1 - yh, yl, x, c)
    next_y = device(z, 1 - yh, 1 - yl, x, c)

    lead = lax.div(ring(z, 3, 8), 2)

    def quarter(j):
        return at(lax.rem(lead + j, 4), QUARTER)

    barrier = pltpu.get_barrier_semaphore()
    peers = (sibling, left, right, across, up, down, other_y, next_y)
    for peer in peers:
        pl.semaphore_signal(barrier, inc=1, device_id=peer, device_id_type=MESH)
    tok_in = pltpu.make_async_copy(tok_h, tok, in_sem.at[0])
    gain_in = pltpu.make_async_copy(gain_h, gain, in_sem.at[1])
    dm_in = pltpu.make_async_copy(dm_h, dm, in_sem.at[2])
    for copy in (tok_in, gain_in, dm_in):
        copy.start()

    def remote(src, dst, send_sem, recv_sem, to):
        return pltpu.make_async_remote_copy(
            src_ref=src, dst_ref=dst, send_sem=send_sem, recv_sem=recv_sem,
            device_id=to, device_id_type=MESH,
        )

    tok_in.wait()
    gain_in.wait()
    values = tok[...].astype(F32)
    scale = lax.rsqrt(jnp.mean(values * values, axis=-1, keepdims=True) + 1e-06)
    normed = values * scale * gain[...]
    mine = at(tensor, ROWS)
    sides = [
        jnp.concatenate(
            [normed[:, (2 * k + h) * HALF : (2 * k + h + 1) * HALF] for k in range(8)], axis=1
        )
        for h in range(2)
    ]
    fn[mine, :SIDE] = jnp.where(yh == 0, sides[1], sides[0]).astype(BF)
    fn[mine, SIDE:] = jnp.where(yh == 0, sides[0], sides[1]).astype(BF)
    dm_in.wait()
    for j in range(4):
        fd[mine, j * QUARTER : (j + 1) * QUARTER] = dm[:, quarter(j)]

    columns = (pl.ds(0, 256), pl.ds(256, 128), pl.ds(384, 128))
    for i, weight in enumerate((wq, wk, wv)):
        for h in range(2):
            for k in range(8):
                pltpu.make_async_copy(
                    weight.at[at(2 * k + lax.rem(yh + 1 + h, 2), HALF), :],
                    w.at[pl.ds((8 * h + k) * HALF, HALF), columns[i]],
                    in_sem.at[3 + i],
                ).start()
    for j in range(4):
        pltpu.make_async_copy(
            wo.at[:, quarter(j)], wout.at[:, pl.ds(j * QUARTER, QUARTER)], in_sem.at[6]
        ).start()
    pl.semaphore_wait(barrier, len(peers))

    def block(dx, dy, core):
        return (yl if dy == 0 else 1 - yl) * 8 + ring(x, dx, 4) * 2 + core

    class Gather:
        order = ((0, 0), (-1, 0), (1, 0), (0, 1), (2, 0), (-1, 1), (1, 1), (2, 1))

        def __init__(self, full, a, first_column, columns):
            self.full, self.a = full, a
            self.columns = pl.ds(first_column, columns)

        def copy(self, i, rows, to):
            ref = self.full.at[rows, self.columns]
            return remote(ref, ref, ag_s.at[self.a, i], ag_r.at[self.a, i], to)

        def whole(self, dx, dy, core=c):
            return at(block(dx, dy, core), ROWS)

        def piece(self, dx, half):
            return at(block(dx, 0, c) * 2 + half, ROWS // 2)

        def to_sibling(self, i):
            self.copy(8 + i, self.whole(*self.order[i]), sibling).start()

        def step1(self):
            self.copy(0, self.whole(0, 0), right).start()
            self.copy(1, self.whole(0, 0), left).start()
            self.copy(2, self.whole(0, 0), across).start()
            self.to_sibling(0)

        def step2(self):
            self.copy(0, self.whole(-1, 0), right).wait_recv()
            self.copy(3, self.piece(-1, 0), right).start()
            self.copy(1, self.whole(1, 0), left).wait_recv()
            self.copy(4, self.piece(1, 1), left).start()
            self.copy(2, self.whole(0, 1), across).wait_recv()
            self.copy(5, self.whole(0, 1), right).start()
            self.copy(6, self.whole(0, 1), left).start()
            for i in (1, 2, 3):
                self.to_sibling(i)

        def step3(self):
            self.copy(3, self.piece(2, 0), right).wait_recv()
            self.copy(4, self.piece(2, 1), left).wait_recv()
            self.copy(7, self.whole(2, 0), across).start()
            self.to_sibling(4)

        def step4(self):
            self.copy(5, self.whole(-1, 1), right).wait_recv()
            self.to_sibling(5)
            self.copy(6, self.whole(1, 1), left).wait_recv()
            self.to_sibling(6)
            self.copy(7, self.whole(2, 1), across).wait_recv()
            self.to_sibling(7)

        def end(self):
            for i in range(8):
                self.copy(8 + i, self.whole(*self.order[i], 1 - c), sibling).wait_recv()

        def sent(self):
            for i, to in ((0, right), (1, left), (2, across), (5, right), (6, left), (7, across)):
                self.copy(i, self.whole(0, 0), to).wait_send()
            self.copy(3, self.piece(0, 0), right).wait_send()
            self.copy(4, self.piece(0, 0), left).wait_send()
            for i in range(8):
                self.copy(8 + i, self.whole(0, 0), sibling).wait_send()

    n = [Gather(fn, t, t * THIRD, THIRD) for t in range(3)]
    d_parts = ((0, 2 * QUARTER), (2 * QUARTER, QUARTER), (3 * QUARTER, QUARTER))
    d = [Gather(fd, 3 + t, *d_parts[t]) for t in range(3)]

    pieces = ((0, THIRD), (THIRD, SIDE - THIRD))

    def from_next(i):
        ref = (at(c, SEQ // 2), pl.ds(*pieces[i]))
        return remote(fn.at[ref], fx.at[ref], hi_s.at[i], hi_r.at[i], next_y)

    def from_sibling(i):
        ref = fx.at[at(c, SEQ // 2), pl.ds(*pieces[i])]
        return remote(ref, ref, hi_s.at[2 + i], hi_r.at[2 + i], sibling)

    def third(t):
        return slice(t * THIRD, (t + 1) * THIRD)

    def project(t):
        term = dot(fn[:, third(t)], w[third(t), :])
        if t == 0:
            acc[...] = term
        elif t == 1:
            acc[...] += term
        else:
            qkv[...] = (acc[...] + term).astype(BF)

    n[0].step1()
    n[1].step1()

    n[0].step2()
    n[2].step1()
    n[0].step3()
    n[1].step2()
    d[0].step1()
    n[0].step4()
    n[1].step3()
    n[2].step2()
    n[0].end()
    for i, weight in enumerate((wq, wk, wv)):
        pltpu.make_async_copy(weight, w.at[:, columns[i]], in_sem.at[3 + i]).wait()
    project(0)
    from_next(0).start()
    n[1].step4()
    d[1].step1()
    n[2].step3()
    n[1].end()
    from_next(1).start()
    project(1)
    d[0].step2()
    n[2].step4()
    d[2].step1()
    n[2].end()
    project(2)

    blocks = ((0, 256), (256, 512))

    def attend(h):
        for lo, hi in blocks:
            q = qkv[lo:hi, h * HEAD : (h + 1) * HEAD]
            scores = dot(q, qkv[:hi, 256:384], ABT)
            th = jnp.tanh(scores * (SCALE / CAP))
            row = lax.broadcasted_iota(jnp.int32, (256, hi), 0) + lo
            col = lax.broadcasted_iota(jnp.int32, (256, hi), 1)
            weight = jnp.where(row >= col, jnp.exp(CAP * th), 0.0)
            p = weight * (1.0 / jnp.sum(weight, axis=-1, keepdims=True))
            probs[h, lo:hi, :hi] = p
            slope[h, lo:hi, :hi] = p * ((1.0 - th * th) * SCALE)
            ctx[lo:hi, h * HEAD : (h + 1) * HEAD] = dot(
                p.astype(BF), qkv[:hi, 384:512]
            ).astype(BF)

    attend(0)
    d[0].step3()
    d[1].step2()
    attend(1)
    ctx_t[...] = ctx[...].T

    class Scatter:
        moves = (
            (2, 1, 0, None, across),
            (1, 1, 1, None, right),
            (-1, 1, 2, None, left),
            (2, 0, 3, 0, right),
            (2, 0, 3, 1, left),
            (1, 0, 4, None, right),
            (-1, 0, 5, None, left),
            (0, 1, 6, None, across),
        )

        def __init__(self, a, t):
            self.a, self.t = a, t
            self.part, self.far = part.at[a, t], far_in.at[a, t]

        def chip(self, dx, dy):
            return (yl if dy == 0 else 1 - yl) * 4 + ring(x, dx, 4)

        def sib_copy(self):
            a, t = self.a, self.t
            return remote(
                part.at[a, t, :, 1 - c], sib_in.at[a, t], sib_s.at[a, t], sib_r.at[a, t], sibling
            )

        def copy(self, i):
            dx, dy, slot, half, to = self.moves[i]
            src, dst = self.part.at[self.chip(dx, dy), c], self.far.at[slot]
            if half is not None:
                rows = pl.ds(half * (ROWS // 2), ROWS // 2)
                src, dst = src.at[rows], dst.at[rows]
            return remote(src, dst, far_s.at[self.a, self.t, i], far_r.at[self.a, self.t, i], to)

        def add(self, dx, dy, slots, rows=slice(0, ROWS)):
            a, t, k = self.a, self.t, self.chip(dx, dy)
            total = part[a, t, k, c, rows].astype(F32)
            for slot in slots:
                total = total + far_in[a, t, slot, rows].astype(F32)
            part[a, t, k, c, rows] = total.astype(BF)

        def start(self, term):
            part[self.a, self.t] = term.astype(BF).reshape(8, 2, ROWS, THIRD)
            self.sib_copy().start()

        def spread(self):
            a, t = self.a, self.t
            self.sib_copy().wait()

            def one(k, carry):
                part[a, t, k, c] = part[a, t, k, c] + sib_in[a, t, k]
                return carry

            lax.fori_loop(0, 8, one, 0)
            for i in range(3):
                self.copy(i).start()

        def middle(self):
            self.copy(0).wait_recv()
            self.add(2, 0, (0,))
            self.copy(3).start()
            self.copy(4).start()
            self.copy(1).wait_recv()
            self.copy(2).wait_recv()
            self.add(0, 1, (1, 2))
            self.copy(7).start()

        def late(self):
            self.copy(3).wait_recv()
            self.add(1, 0, (3,), slice(0, ROWS // 2))
            self.copy(5).start()
            self.copy(4).wait_recv()
            self.add(-1, 0, (3,), slice(ROWS // 2, ROWS))
            self.copy(6).start()

        def total(self):
            a, t = self.a, self.t
            out = part[a, t, self.chip(0, 0), c].astype(F32)
            for i, slot in ((5, 4), (6, 5), (7, 6)):
                self.copy(i).wait_recv()
                out = out + far_in[a, t, slot].astype(F32)
            return out

        def sent(self):
            for i in range(8):
                self.copy(i).wait_send()

    m = [Scatter(0, t) for t in range(3)]
    g = [Scatter(1, t) for t in range(3)]

    away = (4, 3, 3, 2, 2, 1, 1)

    def chunk_o(k):
        return lax.rem(lax.div(k, 2) + 4 - lead, 4) * 2 + lax.rem(k, 2)

    def chunk_i(k):
        return k

    class Chain:
        def __init__(self, grad, recv, send_sem, recv_sem, half, chunk):
            self.grad, self.recv, self.send_sem, self.recv_sem = grad, recv, send_sem, recv_sem
            self.half, self.chunk = half, chunk

        def place(self, i, way, distance):
            part_of = way if i % 2 == 0 else 1 - way
            k = self.chunk(ring(z, distance * (1 - 2 * way), 8))
            return at(k * 2 + part_of, self.half)

        def copy(self, i, way):
            return remote(
                self.grad.at[self.place(i, way, away[i]), :], self.recv.at[i, way],
                self.send_sem.at[i, way], self.recv_sem.at[i, way], (up, down)[way],
            )

        def arrive(self, i, way):
            self.copy(i, way).wait_recv()
            here = self.place(i, way, away[i] - 1)
            self.grad[here, :] = self.grad[here, :] + self.recv[i, way]

        def start(self):
            for i in range(2):
                for way in range(2):
                    self.copy(i, way).start()

        def step(self, i):
            for way in range(2):
                self.arrive(i - 2, way)
                self.copy(i, way).start()

        def end(self):
            for i in (5, 6):
                for way in range(2):
                    self.arrive(i, way)

        def sent(self):
            for i in range(7):
                for way in range(2):
                    self.copy(i, way).wait_send()

    zo = Chain(grad_o, recv_o, zo_s, zo_r, HALF, chunk_o)
    zq = Chain(grad_i.at[0], recv_i.at[0], zi_s.at[0], zi_r.at[0], HALF // 2, chunk_i)
    zk = Chain(grad_i.at[1], recv_i.at[1], zi_s.at[1], zi_r.at[1], HALF // 2, chunk_i)

    def grad_out(t):
        first, size = d_parts[t]
        cols = slice(first, first + size)
        grad_o[cols, :] = dot(ctx_t[...], fd[:, cols]).astype(BF).T

    def back_out(t):
        first, size = d_parts[t]
        cols = slice(first, first + size)
        term = dot(fd[:, cols], wout[:, cols], ABT)
        if t == 0:
            acc[:, :QC] = term
        elif t == 1:
            acc[:, :QC] += term
        else:
            dctx[...] = (acc[:, :QC] + term).astype(BF)

    pltpu.make_async_copy(wo, wout, in_sem.at[6]).wait()
    d[2].step2()
    d[0].step4()
    d[1].step3()
    for t in range(3):
        m[t].start(dot(ctx[...], wout[:, third(t)]))
    d[0].end()
    grad_out(0)
    zo.start()
    back_out(0)
    d[1].step4()
    d[2].step3()
    m[0].spread()
    d[1].end()
    grad_out(1)
    back_out(1)
    m[1].spread()
    zo.step(2)
    d[2].step4()
    m[2].spread()
    d[2].end()
    grad_out(2)
    zo.step(3)
    back_out(2)

    def pair_copy(i):
        cols = (pl.ds(0, 128), pl.ds(128, 128), pl.ds(256, 256))[i]
        return remote(
            dqkv.at[:, cols], dqkv_x.at[:, cols], y_s.at[2 + i], y_r.at[2 + i], other_y
        )

    acc[...] = jnp.zeros_like(acc)

    def attend_back(h):
        for lo, hi in blocks:
            heads = slice(h * HEAD, (h + 1) * HEAD)
            d_ctx = dctx[lo:hi, heads]
            p = probs[h, lo:hi, :hi]
            d_p = dot(d_ctx, qkv[:hi, 384:512], ABT)
            inner = jnp.sum(p * d_p, axis=-1, keepdims=True)
            d_s = (slope[h, lo:hi, :hi] * (d_p - inner)).astype(BF)
            dqkv[lo:hi, heads] = dot(d_s, qkv[:hi, 256:384]).astype(BF)
            acc[:hi, 256:384] += dot(d_s, qkv[lo:hi, heads], ATB)
            acc[:hi, 384:512] += dot(p.astype(BF), d_ctx, ATB)
        pair_copy(h).start()

    attend_back(0)
    zo.step(4)
    attend_back(1)
    dqkv[:, 256:512] = acc[:, 256:512].astype(BF)
    pair_copy(2).start()
    from_next(0).wait_recv()
    from_sibling(0).start()

    def back_in(t):
        g[t].start(dot(dqkv[...], w[third(t), :], ABT))

    back_in(0)
    zo.step(5)
    back_in(1)
    m[0].middle()
    back_in(2)
    zo.step(6)
    from_next(1).wait_recv()
    from_sibling(1).start()
    m[1].middle()
    g[0].spread()
    m[2].middle()
    g[1].spread()
    g[2].spread()
    for i in range(2):
        from_sibling(i).wait_recv()

    def grad_in(which):
        cols = slice(which * QC, (which + 1) * QC)
        own_t = dqkv[:, cols].T
        pair_t = dqkv_x[:, cols].T
        term = dot(own_t, fn[:, SIDE:]) + dot(pair_t, fx[...])
        grad_i[which] = term.astype(BF).T

    pair_copy(0).wait_recv()
    pair_copy(1).wait_recv()
    grad_in(0)
    zq.start()
    m[0].late()
    m[1].late()
    zq.step(2)
    m[2].late()
    zq.step(3)
    pair_copy(2).wait_recv()
    grad_in(1)
    zk.start()
    zq.step(4)

    def keep(h):
        return at(chunk_o(z) * 2 + h, HALF)

    zo.end()
    zk.step(2)
    g[0].middle()
    zq.step(5)
    g[1].middle()
    zk.step(3)
    g[2].middle()
    zq.step(6)
    y_copy = remote(grad_o.at[keep(1 - yh), :], recv_y, y_s.at[0], y_r.at[0], other_y)
    y_copy.start()
    g[0].late()
    zk.step(4)
    for t in range(3):
        mix_sum[:, third(t)] = m[t].total()
    for j in range(4):
        mixed[:, quarter(j)] = (
            tok[:, quarter(j)].astype(F32) + mix_sum[:, j * QUARTER : (j + 1) * QUARTER]
        ).astype(BF)
    mixed_out = pltpu.make_async_copy(mixed, mixed_o, out_sem.at[0])
    mixed_out.start()
    g[1].late()
    zk.step(5)
    g[2].late()
    for gather in n + d:
        gather.sent()
    for stream in m:
        stream.sent()
    zo.sent()
    zk.step(6)
    y_copy.wait()
    dwo[...] = grad_o[keep(yh), :].astype(F32) + recv_y[...].astype(F32)
    dwo_out = pltpu.make_async_copy(dwo, dwo_o, out_sem.at[5])
    dwo_out.start()
    zq.end()
    dwq[...] = grad_i[0, at(z, HALF), :].astype(F32)
    dwq_out = pltpu.make_async_copy(dwq, dwq_o, out_sem.at[2])
    dwq_out.start()

    sums = [g[t].total() for t in range(3)]
    summed = jnp.concatenate(sums, axis=1)
    first = jnp.where(yh == 0, summed[:, SIDE:], summed[:, :SIDE])
    second = jnp.where(yh == 0, summed[:, :SIDE], summed[:, SIDE:])
    d_normed = jnp.concatenate(
        [
            side[:, k * HALF : (k + 1) * HALF]
            for k in range(8)
            for side in (first, second)
        ],
        axis=1,
    )
    upstream = gain[...] * d_normed
    values = tok[...].astype(F32)
    scale = lax.rsqrt(jnp.mean(values * values, axis=-1, keepdims=True) + 1e-06)
    back_norm = scale * upstream - values * (scale * scale * scale) * jnp.mean(
        upstream * values, axis=-1, keepdims=True
    )
    dtok[...] = (dm[...].astype(F32) + back_norm).astype(BF)
    dtok_out = pltpu.make_async_copy(dtok, dtok_o, out_sem.at[1])
    dtok_out.start()

    zk.end()
    dwk[...] = grad_i[1, at(z, HALF), :HEAD].astype(F32)
    dwv[...] = grad_i[1, at(z, HALF), HEAD:].astype(F32)
    dwk_out = pltpu.make_async_copy(dwk, dwk_o, out_sem.at[3])
    dwk_out.start()
    dwv_out = pltpu.make_async_copy(dwv, dwv_o, out_sem.at[4])
    dwv_out.start()

    for stream in g:
        stream.sent()
    zq.sent()
    zk.sent()
    for i in range(2):
        from_next(i).wait_send()
        from_sibling(i).wait_send()
    for i in range(3):
        pair_copy(i).wait_send()
    for copy in (mixed_out, dtok_out, dwq_out, dwk_out, dwv_out, dwo_out):
        copy.wait()


def hand_out(*refs):
    sources, results, held, sem = refs[:6], refs[6:12], refs[12:18], refs[18]
    loads = [
        pltpu.make_async_copy(source, ref, sem.at[0, i])
        for i, (source, ref) in enumerate(zip(sources, held))
    ]
    stores = [
        pltpu.make_async_copy(ref, result, sem.at[1, i])
        for i, (ref, result) in enumerate(zip(held, results))
    ]
    for load in loads:
        load.start()
    for load, store in zip(loads, stores):
        load.wait()
        store.start()
    for store in stores:
        store.wait()


def on_device(tokens, norm_gain, w_query, w_key, w_value, w_output, d_mixed):
    hbm = pl.BlockSpec(memory_space=pltpu.HBM)
    dma = pltpu.SemaphoreType.DMA
    results = (
        jax.ShapeDtypeStruct((ROWS, D), BF),
        jax.ShapeDtypeStruct((ROWS, D), BF),
        jax.ShapeDtypeStruct((HALF, QC), F32),
        jax.ShapeDtypeStruct((HALF, HEAD), F32),
        jax.ShapeDtypeStruct((HALF, HEAD), F32),
        jax.ShapeDtypeStruct((HALF, QC), F32),
    )
    made = pl.pallas_call(
        kernel,
        out_shape=results,
        in_specs=[hbm] * 7,
        out_specs=(hbm,) * 6,
        scratch_shapes=[
            pltpu.VMEM((ROWS, D), BF),
            pltpu.VMEM((D,), F32),
            pltpu.VMEM((ROWS, D), BF),
            *(pltpu.VMEM(r.shape, r.dtype) for r in results),
            pltpu.VMEM((ROWS, D), F32),
            pltpu.VMEM((SEQ, D), BF),
            pltpu.VMEM((SEQ, D), BF),
            pltpu.VMEM((SEQ, SIDE), BF),
            pltpu.VMEM((D, 512), BF),
            pltpu.VMEM((QC, D), BF),
            pltpu.VMEM((SEQ, 512), BF),
            pltpu.VMEM((SEQ, QC), BF),
            pltpu.VMEM((QC, SEQ), BF),
            pltpu.VMEM((SEQ, QC), BF),
            pltpu.VMEM((SEQ, 512), BF),
            pltpu.VMEM((SEQ, 512), BF),
            pltpu.VMEM((SEQ, 512), F32),
            pltpu.VMEM((2, SEQ, SEQ), F32),
            pltpu.VMEM((2, SEQ, SEQ), F32),
            pltpu.VMEM((D, QC), BF),
            pltpu.VMEM((2, SIDE, QC), BF),
            pltpu.VMEM((7, 2, HALF, QC), BF),
            pltpu.VMEM((2, 7, 2, HALF // 2, QC), BF),
            pltpu.VMEM((HALF, QC), BF),
            pltpu.VMEM((2, 3, 8, 2, ROWS, THIRD), BF),
            pltpu.VMEM((2, 3, 8, ROWS, THIRD), BF),
            pltpu.VMEM((2, 3, 7, ROWS, THIRD), BF),
            dma((7,)),
            dma((6,)),
            dma((6, 16)),
            dma((6, 16)),
            dma((4,)),
            dma((4,)),
            dma((7, 2)),
            dma((7, 2)),
            dma((2, 7, 2)),
            dma((2, 7, 2)),
            dma((5,)),
            dma((5,)),
            dma((2, 3)),
            dma((2, 3)),
            dma((2, 3, 8)),
            dma((2, 3, 8)),
        ],
        compiler_params=pltpu.CompilerParams(
            collective_id=0, has_side_effects=True, vmem_limit_bytes=64 * 2**20 - 2**17
        ),
        cost_estimate=pl.CostEstimate(
            flops=12 * 10**9, bytes_accessed=10**7, transcendentals=10**6
        ),
    )(tokens, norm_gain, w_query, w_key, w_value, w_output, d_mixed)
    mixed, d_tokens, dw_query, dw_key, dw_value, dw_out_t = pl.pallas_call(
        hand_out,
        out_shape=results,
        in_specs=[hbm] * 6,
        out_specs=(hbm,) * 6,
        scratch_shapes=[pltpu.VMEM(r.shape, r.dtype) for r in results] + [dma((2, 6))],
    )(*made)
    return (mixed, d_tokens, dw_query, dw_key, dw_value, dw_out_t.T)


def solution(mesh):
    return jax.shard_map(
        on_device,
        mesh=mesh,
        in_specs=(
            P(("dp", "tensor"), None),
            P(),
            P(None, "tensor"),
            P(None, "tensor"),
            P(None, "tensor"),
            P("tensor", None),
            P(("dp", "tensor"), None),
        ),
        out_specs=(
            P(("dp", "tensor"), None),
            P(("dp", "tensor"), None),
            P("dp", "tensor"),
            P("dp", "tensor"),
            P("dp", "tensor"),
            P("tensor", "dp"),
        ),
        check_vma=False,
    )
```
